128 devices in a mesh: section: 2 (over core), et: 2 (over x_hi), dp: 32 (over z, y, x_lo).
Axes of the slice: x: 4 (x_hi: 2, x_lo: 2; x = x_hi * 2 + x_lo), y: 4, z: 4, core: 2. Of those that a mesh axis runs over, the one named last changes fastest.
Arguments:
- layer_inputs: bfloat16 [2, 1, 8192, 2048], P('section', None, ('dp', 'et')), may hold values from -6 to 6
- out_grad: bfloat16 [1, 8192, 2048], P(None, ('dp', 'et')), may hold values from -6 to 6
- w_gate: bfloat16 [2, 2048, 7168], P('section', None, 'et'), may hold values from -0.125 to 0.125
- w_up: bfloat16 [2, 2048, 7168], P('section', None, 'et'), may hold values from -0.125 to 0.125
- w_down: bfloat16 [2, 2048, 7168], P('section', None, 'et'), may hold values from -0.0625 to 0.0625
- slot_token: int32 [2, 1, 4096], P('section', None, 'dp'), may hold values from -1 to 255, as said below
- slot_gate: float32 [2, 1, 4096], P('section', None, 'dp'), may hold values from 0.1 to 0.9
Outputs:
- in_grad: bfloat16 [2, 1, 8192, 2048], P('section', None, ('dp', 'et'))
- gate_w_grad: bfloat16 [2, 2048, 7168], P('section', 'dp', 'et')
- up_w_grad: bfloat16 [2, 2048, 7168], P('section', 'dp', 'et')
- down_w_grad: bfloat16 [2, 2048, 7168], P('section', 'dp', 'et')
- gate_value_grad: float32 [2, 1, 4096], P('section', None, 'dp')
The draws below stay inside these ranges and needn't reach their ends.
Inputs may be any that keep to these rules, and one draw needn't show every extreme that they name: `slot_token`: each layout (one section, micro-batch and replica) holds distinct tokens of its replica in rising order in its first slots and -1 in the rest; from 64 to 128 slots are live, and in every draw some layout is full.
All inputs are finite; a program needn't handle non-finite values.
Results may differ from the reference program's by a relative error of at most 0.024.
Values may be sent and summed in bfloat16 or wider, within the bound.
A program may use at most 320 MiB of HBM per device.

```python
import jax
import jax.numpy as jnp
from jax import lax

D = 2048
FF = 7168
MB = 1
TOK = 256
SECTIONS = 2
SLOTS = 128
TOKENS = 8192
ALL_SLOTS = 4096
N_ET = 2
N_DP = 32


def draw_slot_token(key, part):
    layout_count = SECTIONS * MB * (ALL_SLOTS // SLOTS)
    key_list = jax.random.split(key, layout_count + 1)
    full_index = jax.random.randint(key_list[layout_count], (), 0, layout_count)

    def layout(sub_key, position):
        pick_key, live_key = jax.random.split(sub_key)
        chosen = jnp.sort(jax.random.permutation(pick_key, TOK)[:SLOTS])
        live_count = jax.random.randint(live_key, (), SLOTS // 2, SLOTS + 1)
        live_count = jnp.where(position == full_index, SLOTS, live_count)
        slot_place = jnp.arange(SLOTS)
        return jnp.where(slot_place < live_count, chosen, -1).astype(jnp.int32)
    drawn = jax.vmap(layout)(key_list[:layout_count], jnp.arange(layout_count))
    return drawn.reshape(SECTIONS, MB, ALL_SLOTS)


def block_levels(key, shape, cuts, least, high):
    level, own = 1.0, jax.random.fold_in(key, 6)
    for dim, parts in cuts:
        draws = jnp.exp(jax.random.uniform(jax.random.fold_in(own, dim), (parts,), jnp.float32, least / len(cuts), high / len(cuts)))
        level = level * jnp.repeat(draws, shape[dim] // parts).reshape([-1 if axis == dim else 1 for axis in range(len(shape))])
    return level


def centred(own_key, shape, spread, reach, cuts=(), dtype=jnp.bfloat16):
    entries = jax.random.normal(own_key, shape, jnp.float32) * spread
    if len(cuts) > 0:
        entries = block_levels(own_key, shape, cuts, -0.22, 0.18) * entries
    return jnp.clip(entries, min=-reach, max=reach).astype(dtype)


def setup_inputs(seed: int = 0) -> dict:
    arg_keys = jax.random.split(jax.random.key(seed), 8)
    return {
        "layer_inputs": centred(arg_keys[0], (SECTIONS, MB, TOKENS, D), 1.0, 6.0, ((0, 2), (2, 64))),
        "out_grad": centred(arg_keys[1], (MB, TOKENS, D), 1.0, 6.0, ((1, 64),)),
        "w_gate": centred(arg_keys[2], (SECTIONS, D, FF), D ** -0.5, 0.125, ((0, 2), (2, 2))),
        "w_up": centred(arg_keys[3], (SECTIONS, D, FF), D ** -0.5, 0.125, ((0, 2), (2, 2))),
        "w_down": centred(arg_keys[4], (SECTIONS, D, FF), FF ** -0.5, 0.0625, ((0, 2), (2, 2))),
        "slot_token": draw_slot_token(jax.random.fold_in(arg_keys[7], 71), 0),
        "slot_gate": jnp.clip(0.1 + 0.79999997 * jax.random.uniform(arg_keys[6], (SECTIONS, MB, ALL_SLOTS), jnp.float32) ** block_levels(arg_keys[6], (SECTIONS, MB, ALL_SLOTS), ((0, 2), (2, 32)), -0.2, 0.2), 0.1, 0.9),
    }


def rounded(value):
    return lax.optimization_barrier(value.astype(jnp.bfloat16))


def matmul(left, right):
    return jnp.dot(left.astype(jnp.float32), right.astype(jnp.float32), precision=lax.Precision.HIGHEST)


def slice_backward(x_rows, g_rows, gates, w_one, w_three, w_two):
    pre_gate = matmul(x_rows, w_one)
    pre_up = matmul(x_rows, w_three)
    sigma = jax.nn.sigmoid(pre_gate)
    active = pre_gate * sigma
    hidden = rounded(active * pre_up)
    back_hidden = matmul(g_rows, w_two)
    gate_part = jnp.sum(hidden.astype(jnp.float32) * back_hidden, axis=1)
    scaled_back = gates[:, None] * back_hidden
    grad_pre_gate = rounded(scaled_back * pre_up * sigma * (1.0 + pre_gate * (1.0 - sigma)))
    grad_pre_up = rounded(scaled_back * active)
    scaled_rows = rounded(gates[:, None] * g_rows.astype(jnp.float32))
    grad_one = matmul(x_rows.T, grad_pre_gate)
    grad_three = matmul(x_rows.T, grad_pre_up)
    grad_two = matmul(scaled_rows.T, hidden)
    rows_back = rounded(matmul(grad_pre_gate, w_one.T) + matmul(grad_pre_up, w_three.T))
    return rows_back, gate_part, grad_one, grad_three, grad_two


def replica_backward(x_rep, g_rep, slots, gates, w_one, w_three, w_two):
    live_mask = slots >= 0
    safe_slots = jnp.clip(slots, 0, TOK - 1).astype(jnp.int32)
    x_rows = jnp.where(live_mask[:, None], x_rep[safe_slots], jnp.zeros((), jnp.bfloat16)).astype(jnp.bfloat16)
    g_rows = jnp.where(live_mask[:, None], g_rep[safe_slots], jnp.zeros((), jnp.bfloat16)).astype(jnp.bfloat16)
    group_width = FF // N_ET

    def per_slice(group_index):
        start = group_index * group_width
        piece_one = lax.dynamic_slice_in_dim(w_one, start, group_width, 1)
        piece_three = lax.dynamic_slice_in_dim(w_three, start, group_width, 1)
        piece_two = lax.dynamic_slice_in_dim(w_two, start, group_width, 1)
        return slice_backward(x_rows, g_rows, gates, piece_one, piece_three, piece_two)

    rows_back, gate_parts, grad_one, grad_three, grad_two = lax.map(per_slice, jnp.arange(N_ET).astype(jnp.int32))
    rows_total = jnp.sum(rows_back.astype(jnp.float32), axis=0)
    token_back = jnp.zeros((TOK, D), jnp.float32).at[safe_slots].add(
        jnp.where(live_mask[:, None], rows_total, jnp.zeros((), jnp.float32)))
    in_grad_rep = (g_rep.astype(jnp.float32) + token_back).astype(jnp.bfloat16)
    gate_grad = jnp.sum(gate_parts, axis=0)

    def joined(stacked):
        return jnp.moveaxis(stacked, 0, 1).reshape(D, FF)

    return in_grad_rep, gate_grad, (joined(grad_one), joined(grad_three), joined(grad_two))


def reference(layer_inputs, out_grad, w_gate, w_up, w_down, slot_token, slot_gate):
    incoming = out_grad.reshape(MB, N_DP, TOK, D)
    segment_in_grads = [None] * SECTIONS
    segment_gate_grads = [None] * SECTIONS
    segment_weight_grads = [None] * SECTIONS
    for segment_index in range(SECTIONS - 1, -1, -1):
        inputs_here = layer_inputs[segment_index].reshape(MB, N_DP, TOK, D).swapaxes(0, 1)
        grads_here = incoming.swapaxes(0, 1)
        slots_here = slot_token[segment_index].reshape(MB, N_DP, SLOTS).swapaxes(0, 1)
        gates_here = slot_gate[segment_index].reshape(MB, N_DP, SLOTS).swapaxes(0, 1)
        weight_one = w_gate[segment_index]
        weight_three = w_up[segment_index]
        weight_two = w_down[segment_index]

        def per_replica(totals, pieces):
            x_rep, g_rep, slot_rep, gate_rep = pieces
            replica_sum = [jnp.zeros((D, FF), jnp.float32) for _ in range(3)]
            backs = []
            gate_list = []
            for micro_index in range(MB):
                token_grad, gate_grad, grads = replica_backward(
                    x_rep[micro_index], g_rep[micro_index], slot_rep[micro_index],
                    gate_rep[micro_index], weight_one, weight_three, weight_two)
                backs.append(token_grad)
                gate_list.append(gate_grad)
                replica_sum = [total + piece for total, piece in zip(replica_sum, grads)]
            new_totals = tuple(total + rounded(piece).astype(jnp.float32) for total, piece in zip(totals, replica_sum))
            return new_totals, (jnp.stack(backs), jnp.stack(gate_list))

        start_totals = tuple(jnp.zeros((D, FF), jnp.float32) for _ in range(3))
        totals, (backs, gate_stack) = lax.scan(per_replica, start_totals, (inputs_here, grads_here, slots_here, gates_here))
        incoming = backs.swapaxes(0, 1)
        segment_in_grads[segment_index] = incoming.reshape(MB, TOKENS, D)
        segment_gate_grads[segment_index] = gate_stack.swapaxes(0, 1).reshape(MB, ALL_SLOTS)
        segment_weight_grads[segment_index] = tuple((total * (1.0 / N_DP)).astype(jnp.bfloat16) for total in totals)
    in_grad = jnp.stack(segment_in_grads)
    gate_w_grad = jnp.stack([grads[0] for grads in segment_weight_grads])
    up_w_grad = jnp.stack([grads[1] for grads in segment_weight_grads])
    down_w_grad = jnp.stack([grads[2] for grads in segment_weight_grads])
    gate_value_grad = jnp.stack(segment_gate_grads)
    return (in_grad, gate_w_grad, up_w_grad, down_w_grad, gate_value_grad)
```

```python
import jax
import jax.numpy as jnp
from jax import lax
from jax.sharding import PartitionSpec as P

BF = jnp.bfloat16
F32 = jnp.float32
NY = 4
NZ = 4
NX = 2


def dp_id(z, y, x):
    return z * (NY * NX) + y * NX + x


def shift_pairs(axis, step):
    pairs = []
    for z in range(NZ):
        for y in range(NY):
            for x in range(NX):
                if axis == "z":
                    target = dp_id((z + step) % NZ, y, x)
                elif axis == "y":
                    target = dp_id(z, (y + step) % NY, x)
                else:
                    target = dp_id(z, y, (x + step) % NX)
                pairs.append((dp_id(z, y, x), target))
    return pairs


def shift(value, axis, step):
    return lax.ppermute(value, "dp", shift_pairs(axis, step))


def swap_et(value):
    return lax.ppermute(value, "et", [(0, 1), (1, 0)])


def mm(a, b):
    return jnp.dot(a, b, preferred_element_type=F32)


def mm_rows(a, b):
    return lax.dot_general(a, b, (((0,), (0,)), ((), ())), preferred_element_type=F32)


def mm_hidden(a, b):
    return lax.dot_general(a, b, (((1,), (1,)), ((), ())), preferred_element_type=F32)


def per_device(layer_inputs, out_grad, w_gate, w_up, w_down, slot_token, slot_gate):
    section = lax.axis_index("section")
    et = lax.axis_index("et")
    dp = lax.axis_index("dp")
    pos = {"z": dp // (NY * NX), "y": (dp // NX) % NY, "x": dp % NX}
    x_own = layer_inputs[0, 0]
    g_own = out_grad[0]
    tok = x_own.shape[0]
    slots = slot_token[0, 0]
    gates = slot_gate[0, 0]
    w_one, w_three, w_two = w_gate[0], w_up[0], w_down[0]

    token_ids = jnp.arange(tok, dtype=jnp.int32)
    sel_own = (slots[:, None] == token_ids[None, :] + et * tok).astype(BF)
    sel_other = (slots[:, None] == token_ids[None, :] + (1 - et) * tok).astype(BF)

    x_other = swap_et(x_own)
    g_other = swap_et(g_own)
    x_rows = (mm(sel_own, x_own) + mm(sel_other, x_other)).astype(BF)
    pre_gate = mm(x_rows, w_one)
    pre_up = mm(x_rows, w_three)
    sigma = jax.nn.sigmoid(pre_gate)
    active = pre_gate * sigma
    hidden = (active * pre_up).astype(BF)
    slope = pre_up * sigma * (1.0 + pre_gate * (1.0 - sigma))

    def tick(g_own, g_other):
        g_rows = (mm(sel_own, g_own) + mm(sel_other, g_other)).astype(BF)
        back_hidden = mm(g_rows, w_two)
        gate_part = jnp.sum(hidden.astype(F32) * back_hidden, axis=1)
        scaled_back = gates[:, None] * back_hidden
        grad_pre_gate = (scaled_back * slope).astype(BF)
        grad_pre_up = (scaled_back * active).astype(BF)
        scaled_rows = (gates[:, None] * g_rows.astype(F32)).astype(BF)
        rows_back = (mm_hidden(grad_pre_gate, w_one) + mm_hidden(grad_pre_up, w_three)).astype(BF)
        rows_other = swap_et(rows_back)
        new_own = (g_own.astype(F32) + (mm_rows(sel_own, rows_back) + mm_rows(sel_own, rows_other))).astype(BF)
        new_other = (g_other.astype(F32) + (mm_rows(sel_other, rows_back) + mm_rows(sel_other, rows_other))).astype(BF)
        return gate_part, grad_pre_gate, grad_pre_up, scaled_rows, new_own, new_other

    first = tick(g_own, g_other)
    got_own = lax.ppermute(first[4], "section", [(1, 0)])
    got_other = lax.ppermute(first[5], "section", [(1, 0)])
    last_section = section == 1
    g_own = jnp.where(last_section, g_own, got_own)
    g_other = jnp.where(last_section, g_other, got_other)
    gate_part, grad_pre_gate, grad_pre_up, scaled_rows, new_own, _ = tick(g_own, g_other)
    gate_value = gate_part + swap_et(gate_part)

    slots_n, width = x_rows.shape
    half = hidden.shape[1] // 2

    def regroup(rows):
        return {
            "y": rows.reshape(slots_n, NZ, NY, -1).transpose(2, 0, 1, 3).reshape(NY, slots_n, -1),
            "z": rows.reshape(slots_n, NZ, -1).transpose(1, 0, 2),
        }

    x_parts, s_parts = regroup(x_rows), regroup(scaled_rows)

    def pick(stack, index):
        return lax.dynamic_index_in_dim(stack, index, 0, keepdims=False)

    def gathered(value, axis):
        return [value] + [shift(value, axis, step) for step in (1, 3, 2)]

    def dealt(parts, axis):
        here = pos[axis]
        return [pick(parts, here)] + [
            shift(pick(parts, (here + step) % 4), axis, step) for step in (1, 3, 2)]

    outs = []
    lefts = {"y": {}, "z": {}}
    for axis in ("y", "z"):
        lefts[axis]["x"] = jnp.concatenate(dealt(x_parts[axis], axis), axis=0)
        lefts[axis]["s"] = jnp.concatenate(dealt(s_parts[axis], axis), axis=0)
    for name, value in (("s", hidden), ("x", grad_pre_gate), ("x", grad_pre_up)):
        pieces = []
        for axis, other, lo in (("y", "z", 0), ("z", "y", half)):
            right = jnp.concatenate(gathered(value[:, lo:lo + half], axis), axis=0)
            part = mm_rows(lefts[axis][name], right)
            part = part.astype(BF).reshape(4, -1, half)
            here = pos[other]
            total = pick(part, here).astype(F32)
            for step in (1, 3, 2):
                total = total + shift(pick(part, (here + step) % 4), other, step).astype(F32)
            total = total.astype(BF).reshape(NX, -1, half)
            mine = pick(total, pos["x"]).astype(F32)
            arrived = shift(pick(total, 1 - pos["x"]), "x", 1).astype(F32)
            pieces.append(((mine + arrived) * (1.0 / 32.0)).astype(BF))
        outs.append(jnp.concatenate(pieces, axis=1)[None])
    down, gate, up = outs
    return (new_own[None, None], gate, up, down, gate_value[None, None])


def solution(mesh):
    placed = (
        P("section", None, ("dp", "et"), None),
        P(None, ("dp", "et"), None),
        P("section", None, "et"),
        P("section", None, "et"),
        P("section", None, "et"),
        P("section", None, "dp"),
        P("section", None, "dp"),
    )
    return jax.shard_map(
        per_device,
        mesh=mesh,
        in_specs=placed,
        out_specs=(
            P("section", None, ("dp", "et"), None),
            P("section", "dp", "et"),
            P("section", "dp", "et"),
            P("section", "dp", "et"),
            P("section", None, "dp"),
        ),
        check_vma=False,
    )
```

```python
import jax
import jax.numpy as jnp
from jax import lax
from jax.experimental import pallas as pl
from jax.experimental.pallas import tpu as pltpu
from jax.sharding import PartitionSpec as P

BF = jnp.bfloat16
F32 = jnp.float32
NY, NZ, NX = 4, 4, 2
RING = 4
COLS = 256
MESH = pl.DeviceIdType.MESH


def dot(a, b):
    return jnp.dot(a, b, preferred_element_type=F32)


def dot_nt(a, b):
    return lax.dot_general(a, b, (((1,), (1,)), ((), ())), preferred_element_type=F32)


def body(
    slots_col, slots_row, gates_col, x_hbm, g_hbm, w1_hbm, w3_hbm, w2_hbm,
    in_grad, gate_out, up_out, down_out, value_out,
    w1, w3, w2, x_full, g_full, x_rows, g_rows, x_turned, s_turned,
    active_ref, slope_ref, right, left, rows_sum, rows_mine, rows_theirs, grads_both,
    value_mine, value_theirs,
    load_sem, w2_sem, local_sem, pair_send, pair_recv, hop_send, hop_recv,
    left_send, left_recv, right_send, right_recv, sum_send, sum_recv, x_send, x_recv, ready,
):
    section = lax.axis_index("section")
    et = lax.axis_index("et")
    dp = lax.axis_index("dp")
    z, y, x = dp // (NY * NX), (dp // NX) % NY, dp % NX
    slots_n = slots_row.shape[1]
    tok = x_full.shape[1]
    chunks = w1.shape[0]
    half = chunks // 2
    ring_w2 = w2.shape[0]
    width = w1.shape[1]

    def at_y(step):
        return (section, et, z * (NY * NX) + ((y + step) % NY) * NX + x)

    def at_z(step):
        return (section, et, ((z + step) % NZ) * (NY * NX) + y * NX + x)

    pair = (section, 1 - et, dp)
    sibling = (1 - section, et, dp)
    x_peer = (section, et, z * (NY * NX) + y * NX + (1 - x))
    gather_to = (at_y, at_z)
    reduce_to = (at_z, at_y)
    gather_pos = (y, z)
    reduce_pos = (z, y)

    def remote(src, dst, send, recv, device):
        return pltpu.make_async_remote_copy(
            src_ref=src, dst_ref=dst, send_sem=send, recv_sem=recv,
            device_id=device, device_id_type=MESH)

    def w_load(hbm, ref, c, sem):
        start = pl.multiple_of(c * COLS, COLS)
        return pltpu.make_async_copy(hbm.at[0, :, pl.ds(start, COLS)], ref, sem)

    x_load = pltpu.make_async_copy(x_hbm.at[0, 0], x_full.at[0], local_sem.at[0])
    g_load = pltpu.make_async_copy(g_hbm.at[0], g_full.at[0], local_sem.at[1])
    x_load.start()

    @pl.when(section == 1)
    def _():
        g_load.start()

    @pl.loop(0, chunks)
    def _(c):
        w_load(w1_hbm, w1.at[c], c, load_sem.at[0, c]).start()
        w_load(w3_hbm, w3.at[c], c, load_sem.at[1, c]).start()

    @pl.loop(0, ring_w2)
    def _(c):
        w_load(w2_hbm, w2.at[c], c, w2_sem.at[c]).start()

    barrier = pltpu.get_barrier_semaphore()
    peers = [pair, sibling, x_peer] + [at_y(k) for k in (1, 2, 3)] + [at_z(k) for k in (1, 2, 3)]
    for peer in peers:
        pl.semaphore_signal(barrier, inc=1, device_id=peer, device_id_type=MESH)
    pl.semaphore_wait(barrier, len(peers))

    x_swap = remote(x_hbm.at[0, 0], x_full.at[1], pair_send.at[0], pair_recv.at[0], pair)
    g_swap = remote(g_hbm.at[0], g_full.at[1], pair_send.at[1], pair_recv.at[1], pair)
    x_swap.start()

    @pl.when(section == 1)
    def _():
        g_swap.start()

    token = lax.broadcasted_iota(jnp.int32, (slots_n, 2 * tok), 1)
    token = token + jnp.where(token < tok, et * tok, -et * tok)
    pick = jnp.where(slots_col[...] == token, 1.0, 0.0).astype(BF)
    turned = lax.broadcasted_iota(jnp.int32, (tok, slots_n), 0)
    place = [
        jnp.where(slots_row[...] == turned + et * tok, 1.0, 0.0).astype(BF),
        jnp.where(slots_row[...] == turned + (1 - et) * tok, 1.0, 0.0).astype(BF),
    ]

    def select(both):
        return dot(pick[:, :tok], both[0]) + dot(pick[:, tok:], both[1])

    def turn(rows, into):
        for b in range(width // 128):
            block = rows[:, b * 128:(b + 1) * 128].astype(F32)
            into[b // 4, b % 4] = block.T.astype(BF)

    def deal(which, source):
        copies = []
        for h in range(2):
            own = source.at[:, gather_pos[h]] if h == 0 else source.at[gather_pos[h]]
            left[which, h, :, :, 0:128] = own[...]
            for k in (1, 2, 3):
                there = (gather_pos[h] + k) % RING
                src = source.at[:, there] if h == 0 else source.at[there]
                copy = remote(src, left.at[which, h, :, :, pl.ds(k * 128, 128)],
                              left_send.at[which, h, k - 1], left_recv.at[which, h, k - 1], gather_to[h](k))
                copy.start()
                copies.append(copy)
        return copies

    def spread(t):
        copies = []
        for h in range(2):
            for k in (2, 1, 3):
                copy = remote(right.at[t, pl.ds(half * h, half), pl.ds(0, slots_n), :],
                              right.at[t, pl.ds(half * h, half), pl.ds(k * slots_n, slots_n), :],
                              right_send.at[t, h, k - 1], right_recv.at[t, h, k - 1], gather_to[h](k))
                copy.start()
                copies.append(copy)
        return copies

    x_load.wait()
    x_swap.wait_recv()
    x_rows[...] = select(x_full).astype(BF)

    @pl.loop(0, chunks)
    def _(c):
        w_load(w1_hbm, w1.at[c], c, load_sem.at[0, c]).wait()
        w_load(w3_hbm, w3.at[c], c, load_sem.at[1, c]).wait()
        pre_gate = dot(x_rows[...], w1[c])
        pre_up = dot(x_rows[...], w3[c])
        sigma = jax.nn.sigmoid(pre_gate)
        active = pre_gate * sigma
        active_ref[c] = active
        slope_ref[c] = pre_up * sigma * (1.0 + pre_gate * (1.0 - sigma))
        right[0, c, 0:slots_n, :] = (active * pre_up).astype(BF)

    sent = spread(0)
    turn(x_rows[...], x_turned)
    sent += deal(0, x_turned)

    hops = [remote(grads_both.at[i], g_full.at[i], hop_send.at[i], hop_recv.at[i], sibling) for i in range(2)]

    @pl.when(section == 1)
    def _():
        g_load.wait()
        g_swap.wait_recv()

    @pl.when(section == 0)
    def _():
        hops[0].wait_recv()
        hops[1].wait_recv()

    g_rows[...] = select(g_full).astype(BF)
    rows_sum[...] = jnp.zeros_like(rows_sum)
    value_mine[...] = jnp.zeros_like(value_mine)
    gates = gates_col[...]

    @pl.loop(0, chunks)
    def _(c):
        slot = c % ring_w2
        w_load(w2_hbm, w2.at[slot], c, w2_sem.at[slot]).wait()
        back = dot(g_rows[...], w2[slot])

        @pl.when(c + ring_w2 < chunks)
        def _():
            w_load(w2_hbm, w2.at[slot], c + ring_w2, w2_sem.at[slot]).start()

        product = right[0, c, 0:slots_n, :].astype(F32) * back
        value_mine[...] += product[:, :128] + product[:, 128:]
        scaled = gates * back
        grad_gate = (scaled * slope_ref[c]).astype(BF)
        grad_up = (scaled * active_ref[c]).astype(BF)
        right[1, c, 0:slots_n, :] = grad_gate
        right[2, c, 0:slots_n, :] = grad_up
        rows_sum[...] += dot_nt(w1[c], grad_gate) + dot_nt(w3[c], grad_up)

    rows_mine[...] = rows_sum[...].astype(BF)
    rows_swap = remote(rows_mine, rows_theirs, pair_send.at[2], pair_recv.at[2], pair)
    value_swap = remote(value_mine, value_theirs, pair_send.at[3], pair_recv.at[3], pair)
    rows_swap.start()
    value_swap.start()

    for peer in peers[2:]:
        pl.semaphore_signal(ready, inc=1, device_id=peer, device_id_type=MESH)

    sent += spread(1)
    sent += spread(2)
    turn(gates * g_rows[...].astype(F32), s_turned)
    sent += deal(1, s_turned)

    rows_swap.wait_recv()

    def token_grads(i):
        step = 512
        for b in range(width // step):
            cols = slice(b * step, (b + 1) * step)
            added = dot_nt(place[i], rows_mine[cols, :]) + dot_nt(place[i], rows_theirs[cols, :])
            grads_both[i, :, cols] = (g_full[i, :, cols].astype(F32) + added).astype(BF)

    @pl.when(section == 1)
    def _():
        token_grads(1)
        hops[1].start()

    token_grads(0)

    @pl.when(section == 1)
    def _():
        hops[0].start()

    in_grad[0, 0] = grads_both[0]
    value_swap.wait_recv()
    value_out[0] = jnp.sum((value_mine[...] + value_theirs[...]).T, axis=0, keepdims=True)

    outs = (down_out, gate_out, up_out)
    block = RING * 128

    def left_wait(which):
        for h in range(2):
            for k in (1, 2, 3):
                remote(left.at[which, h, :, :, pl.ds(k * 128, 128)], left.at[which, h, :, :, pl.ds(k * 128, 128)],
                       left_send.at[which, h, k - 1], left_recv.at[which, h, k - 1], gather_to[h](k)).wait_recv()

    def multiply(t, h):
        for k in (1, 3, 2):
            part = right.at[t, pl.ds(half * h, half), pl.ds(k * slots_n, slots_n), :]
            remote(part, part, right_send.at[t, h, k - 1], right_recv.at[t, h, k - 1], gather_to[h](k)).wait_recv()
        which = 1 if t == 0 else 0

        @pl.loop(0, half)
        def _(n):
            c = half * h + n
            a = left[which, h].reshape(block, RING * slots_n)
            w1[c, t * block:(t + 1) * block, :] = dot(a, right[t, c]).astype(BF)

    def sum_copy(t, h, k):
        there = pl.multiple_of(t * block + ((reduce_pos[h] + k) % RING) * 128, 128)
        return remote(w1.at[pl.ds(half * h, half), pl.ds(there, 128), :],
                      w3.at[pl.ds(half * h, half), pl.ds(t * block + k * 128, 128), :],
                      sum_send.at[t, h, k - 1], sum_recv.at[t, h, k - 1], reduce_to[h](k))

    def reduce_start(t, h):
        copies = []
        for k in (2, 1, 3):
            copy = sum_copy(t, h, k)
            copy.start()
            copies.append(copy)
        return copies

    def total(t, h, c, side):
        here = pl.multiple_of(t * block + reduce_pos[h] * 128 + side * 64, 64)
        value = w1[c, pl.ds(here, 64), :].astype(F32)
        for k in (1, 2, 3):
            there = pl.multiple_of(t * block + k * 128 + side * 64, 64)
            value = value + w3[c, pl.ds(there, 64), :].astype(F32)
        return value

    def x_copy(t, h):
        at = (pl.ds(half * h, half), pl.ds(3 * block + t * 64, 64), slice(None))
        return remote(w1.at[at], w3.at[at], x_send.at[t, h], x_recv.at[t, h], x_peer)

    def reduce_end(t, h):
        for k in (1, 3, 2):
            sum_copy(t, h, k).wait_recv()

        @pl.loop(0, half)
        def _(n):
            c = half * h + n
            w1[c, 3 * block + t * 64:3 * block + (t + 1) * 64, :] = total(t, h, c, 1 - x).astype(BF)
        copy = x_copy(t, h)
        copy.start()
        return [copy]

    def finish(t, h):
        x_copy(t, h).wait_recv()
        for n in range(half):
            c = half * h + n
            arrived = w3[c, 3 * block + t * 64:3 * block + (t + 1) * 64, :].astype(F32)
            outs[t][0, :, c * COLS:(c + 1) * COLS] = ((total(t, h, c, x) + arrived) * (1.0 / 32.0)).astype(BF)

    left_wait(1)
    multiply(0, 0)
    pl.semaphore_wait(ready, len(peers) - 2)
    sent += reduce_start(0, 0)
    multiply(0, 1)
    sent += reduce_start(0, 1)
    left_wait(0)
    for h in range(2):
        multiply(1, h)
        sent += reduce_start(1, h)
    for h in range(2):
        sent += reduce_end(0, h)
    for h in range(2):
        multiply(2, h)
        sent += reduce_start(2, h)
    for h in range(2):
        sent += reduce_end(1, h)
    for h in range(2):
        finish(0, h)
    for h in range(2):
        sent += reduce_end(2, h)
    for t in (1, 2):
        for h in range(2):
            finish(t, h)

    for copy in sent:
        copy.wait_send()
    x_swap.wait_send()
    rows_swap.wait_send()
    value_swap.wait_send()

    @pl.when(section == 1)
    def _():
        g_swap.wait_send()
        hops[0].wait_send()
        hops[1].wait_send()


def per_device(layer_inputs, out_grad, w_gate, w_up, w_down, slot_token, slot_gate):
    tok, width = layer_inputs.shape[2:]
    hidden = w_gate.shape[2]
    slots_n = slot_token.shape[2]
    chunks = hidden // COLS
    rows_out = width // (NY * NZ * NX)
    vmem = pl.BlockSpec(memory_space=pltpu.VMEM)
    hbm = pl.BlockSpec(memory_space=pl.ANY)
    sem = pltpu.SemaphoreType.DMA
    grad = jax.ShapeDtypeStruct((1, rows_out, hidden), BF)
    return pl.pallas_call(
        body,
        out_shape=(
            jax.ShapeDtypeStruct((1, 1, tok, width), BF), grad, grad, grad,
            jax.ShapeDtypeStruct((1, 1, slots_n), F32),
        ),
        in_specs=[vmem, vmem, vmem, hbm, hbm, hbm, hbm, hbm],
        out_specs=(vmem,) * 5,
        scratch_shapes=[
            pltpu.VMEM((chunks, width, COLS), BF),
            pltpu.VMEM((chunks, width, COLS), BF),
            pltpu.VMEM((chunks // 2, width, COLS), BF),
            pltpu.VMEM((2, tok, width), BF),
            pltpu.VMEM((2, tok, width), BF),
            pltpu.VMEM((slots_n, width), BF),
            pltpu.VMEM((slots_n, width), BF),
            pltpu.VMEM((RING, RING, 128, slots_n), BF),
            pltpu.VMEM((RING, RING, 128, slots_n), BF),
            pltpu.VMEM((chunks, slots_n, COLS), F32),
            pltpu.VMEM((chunks, slots_n, COLS), F32),
            pltpu.VMEM((3, chunks, RING * slots_n, COLS), BF),
            pltpu.VMEM((2, 2, RING, 128, RING * slots_n), BF),
            pltpu.VMEM((width, slots_n), F32),
            pltpu.VMEM((width, slots_n), BF),
            pltpu.VMEM((width, slots_n), BF),
            pltpu.VMEM((2, tok, width), BF),
            pltpu.VMEM((slots_n, 128), F32),
            pltpu.VMEM((slots_n, 128), F32),
            sem((2, chunks)), sem((chunks // 2,)), sem((2,)),
            sem((4,)), sem((4,)), sem((2,)), sem((2,)),
            sem((2, 2, 3)), sem((2, 2, 3)), sem((3, 2, 3)), sem((3, 2, 3)),
            sem((3, 2, 3)), sem((3, 2, 3)), sem((3, 2)), sem((3, 2)),
            pltpu.SemaphoreType.REGULAR,
        ],
        compiler_params=pltpu.CompilerParams(
            collective_id=0, has_side_effects=True, vmem_limit_bytes=63 * 1024 * 1024),
    )(
        slot_token.reshape(slots_n, 1), slot_token.reshape(1, slots_n), slot_gate.reshape(slots_n, 1),
        layer_inputs, out_grad, w_gate, w_up, w_down,
    )


def solution(mesh):
    placed = (
        P("section", None, ("dp", "et"), None),
        P(None, ("dp", "et"), None),
        P("section", None, "et"),
        P("section", None, "et"),
        P("section", None, "et"),
        P("section", None, "dp"),
        P("section", None, "dp"),
    )
    return jax.shard_map(
        per_device,
        mesh=mesh,
        in_specs=placed,
        out_specs=(
            P("section", None, ("dp", "et"), None),
            P("section", "dp", "et"),
            P("section", "dp", "et"),
            P("section", "dp", "et"),
            P("section", None, "dp"),
        ),
        check_vma=False,
    )
```

```python
import jax
import jax.numpy as jnp
from jax import lax
from jax.experimental import pallas as pl
from jax.experimental.pallas import tpu as pltpu
from jax.sharding import PartitionSpec as P

BF = jnp.bfloat16
F32 = jnp.float32
NY, NZ, NX = 4, 4, 2
RING = 4
COLS = 256
MESH = pl.DeviceIdType.MESH


def dot(a, b):
    return jnp.dot(a, b, preferred_element_type=F32)


def dot_nt(a, b):
    return lax.dot_general(a, b, (((1,), (1,)), ((), ())), preferred_element_type=F32)


def body(
    slots_ref, gates_ref, x_hbm, g_hbm, w1_hbm, w3_hbm, w2_hbm,
    in_grad, gate_out, up_out, down_out, value_out,
    w1, w3, w2, x_full, g_full, x_rows, g_rows, x_turned, s_turned,
    active_ref, slope_ref, right, left, rows_mine, rows_theirs, grads_both,
    value_mine, value_theirs,
    load_sem, w2_sem, local_sem, pair_send, pair_recv, rows_send, rows_recv, hop_send, hop_recv,
    left_send, left_recv, right_send, right_recv, far_send, far_recv, sum_send, sum_recv, x_send, x_recv,
    ready, turn_sem,
):
    section = lax.axis_index("section")
    et = lax.axis_index("et")
    dp = lax.axis_index("dp")
    z, y, x = dp // (NY * NX), (dp // NX) % NY, dp % NX
    slots_n = slots_ref.shape[2]
    tok = x_full.shape[1]
    chunks = w1.shape[0]
    half = chunks // 2
    ring_w2 = w2.shape[0]
    width = w1.shape[1]
    part_of = ((0, (half + 1) // 2), ((half + 1) // 2, half // 2))
    step_a = 1 + 2 * section
    step_b = 3 - 2 * section
    steps = (step_a, step_b)

    def at_y(step):
        return (section, et, z * (NY * NX) + ((y + step) % NY) * NX + x)

    def at_z(step):
        return (section, et, ((z + step) % NZ) * (NY * NX) + y * NX + x)

    pair = (section, 1 - et, dp)
    sibling = (1 - section, et, dp)
    x_peer = (section, et, z * (NY * NX) + y * NX + (1 - x))
    gather_to = (at_y, at_z)
    reduce_to = (at_z, at_y)
    gather_pos = (y, z)
    reduce_pos = (z, y)

    def remote(src, dst, send, recv, device):
        return pltpu.make_async_remote_copy(
            src_ref=src, dst_ref=dst, send_sem=send, recv_sem=recv,
            device_id=device, device_id_type=MESH)

    def w_load(hbm, ref, c, sem):
        start = pl.multiple_of(c * COLS, COLS)
        return pltpu.make_async_copy(hbm.at[0, :, pl.ds(start, COLS)], ref, sem)

    x_load = pltpu.make_async_copy(x_hbm.at[0, 0], x_full.at[0], local_sem.at[0])
    g_load = pltpu.make_async_copy(g_hbm.at[0], g_full.at[0], local_sem.at[1])
    x_load.start()

    @pl.when(section == 1)
    def _():
        g_load.start()

    @pl.loop(0, chunks)
    def _(c):
        w_load(w1_hbm, w1.at[c], c, load_sem.at[0, c]).start()
        w_load(w3_hbm, w3.at[c], c, load_sem.at[1, c]).start()

    @pl.loop(0, ring_w2)
    def _(c):
        w_load(w2_hbm, w2.at[c], c, w2_sem.at[c]).start()

    barrier = pltpu.get_barrier_semaphore()
    near = [x_peer] + [at_y(k) for k in (1, 3)] + [at_z(k) for k in (1, 3)]
    peers = [pair, sibling, at_y(2), at_z(2)] + near
    for peer in peers:
        pl.semaphore_signal(barrier, inc=1, device_id=peer, device_id_type=MESH)
    pl.semaphore_wait(barrier, len(peers))

    x_swap = remote(x_hbm.at[0, 0], x_full.at[1], pair_send.at[0], pair_recv.at[0], pair)
    g_swap = remote(g_hbm.at[0], g_full.at[1], pair_send.at[1], pair_recv.at[1], pair)

    @pl.when(section == 0)
    def _():
        pl.semaphore_wait(turn_sem, 1)

    x_swap.start()

    @pl.when(section == 1)
    def _():
        x_swap.wait_send()
        g_swap.start()

    def down_rows(row):
        return jnp.broadcast_to(row.astype(F32), (slots_n, slots_n)).T

    offsets = (et * tok, (1 - et) * tok)
    slot_rows = down_rows(slots_ref[0]).astype(jnp.int32)
    across = lax.broadcasted_iota(jnp.int32, (slots_n, tok), 1)
    pick = [jnp.where(slot_rows == across + o, 1.0, 0.0).astype(BF) for o in offsets]
    along = lax.broadcasted_iota(jnp.int32, (tok, slots_n), 0)
    place = [jnp.where(slots_ref[0] == along + o, 1.0, 0.0).astype(BF) for o in offsets]

    def deal(which, source):
        copies = []
        for h in range(2):
            def share(pos):
                return source.at[:, pos] if h == 0 else source.at[pos]
            left[which, h, :, :, 0:128] = share(gather_pos[h])[...]
            for k, step in ((2, 2), (1, step_a), (3, step_b)):
                copy = remote(share((gather_pos[h] + step) % RING), left.at[which, h, :, :, pl.ds(k * 128, 128)],
                              left_send.at[which, h, k - 1], left_recv.at[which, h, k - 1], gather_to[h](step))
                copy.start()
                copies.append(copy)
        return copies

    def piece(t, h, p, k):
        start, count = part_of[p]
        return right.at[t, pl.ds(half * h + start, count), pl.ds(k * slots_n, slots_n), :]

    def spread_copy(t, h, d, p):
        return remote(piece(t, h, p, 0), piece(t, h, p, 1 + 2 * d),
                      right_send.at[t, h, d, p], right_recv.at[t, h, d, p], gather_to[h](steps[d]))

    def pass_copy(t, h, d):
        return remote(piece(t, h, d, 1 + 2 * d), piece(t, h, d, 2),
                      far_send.at[t, h, d], far_recv.at[t, h, d], gather_to[h](steps[d]))

    def spread(t):
        copies = []
        for d, p in ((0, 0), (1, 1), (0, 1), (1, 0)):
            for h in range(2):
                copy = spread_copy(t, h, d, p)
                copy.start()
                copies.append(copy)
        return copies

    def pass_on(t):
        for h in range(2):
            for d in range(2):
                spread_copy(t, h, d, d).wait_recv()
                pass_copy(t, h, d).start()

    x_load.wait()
    x_swap.wait_recv()
    for b in range(width // 128):
        cols = slice(b * 128, (b + 1) * 128)
        picked = dot(pick[0], x_full[0, :, cols]) + dot(pick[1], x_full[1, :, cols])
        x_rows[:, cols] = picked.astype(BF)
        x_turned[b // 4, b % 4] = picked.T.astype(BF)
    sent = deal(0, x_turned)

    @pl.loop(0, chunks)
    def _(c):
        w_load(w1_hbm, w1.at[c], c, load_sem.at[0, c]).wait()
        w_load(w3_hbm, w3.at[c], c, load_sem.at[1, c]).wait()
        pre_gate = dot(x_rows[...], w1[c])
        pre_up = dot(x_rows[...], w3[c])
        sigma = jax.nn.sigmoid(pre_gate)
        active = pre_gate * sigma
        active_ref[c] = active
        slope_ref[c] = pre_up * sigma * (1.0 + pre_gate * (1.0 - sigma))
        right[0, c, 0:slots_n, :] = (active * pre_up).astype(BF)

    sent += spread(0)

    blocks = grads_both.shape[0]
    step = width // blocks

    def hop(b):
        return remote(grads_both.at[b], g_full.at[:, :, pl.ds(b * step, step)],
                      hop_send.at[b], hop_recv.at[b], sibling)

    @pl.when(section == 1)
    def _():
        g_swap.wait_send()
        pl.semaphore_signal(turn_sem, inc=1, device_id=sibling, device_id_type=MESH)
        g_load.wait()
        g_swap.wait_recv()

    @pl.when(section == 0)
    def _():
        pass_on(0)

    for b in range(blocks):
        cols = slice(b * step, (b + 1) * step)

        @pl.when(section == 0)
        def _():
            hop(b).wait_recv()

        g_rows[:, cols] = (dot(pick[0], g_full[0, :, cols]) + dot(pick[1], g_full[1, :, cols])).astype(BF)

    value_mine[...] = jnp.zeros_like(value_mine)
    gate_block = down_rows(gates_ref[0])
    gates = jnp.concatenate([gate_block] * (COLS // 128), axis=1)

    @pl.loop(0, chunks)
    def _(c):
        slot = c % ring_w2
        w_load(w2_hbm, w2.at[slot], c, w2_sem.at[slot]).wait()
        back = dot(g_rows[...], w2[slot])

        @pl.when(c + ring_w2 < chunks)
        def _():
            w_load(w2_hbm, w2.at[slot], c + ring_w2, w2_sem.at[slot]).start()

        product = right[0, c, 0:slots_n, :].astype(F32) * back
        value_mine[...] += product[:, :128] + product[:, 128:]
        scaled = gates * back
        right[1, c, 0:slots_n, :] = (scaled * slope_ref[c]).astype(BF)
        right[2, c, 0:slots_n, :] = (scaled * active_ref[c]).astype(BF)

    sent += spread(1)
    sent += spread(2)
    value_swap = remote(value_mine, value_theirs, pair_send.at[2], pair_recv.at[2], pair)
    value_swap.start()

    def rows_swap(b):
        return remote(rows_mine.at[b], rows_theirs.at[b], rows_send.at[b], rows_recv.at[b], pair)

    @pl.loop(0, blocks)
    def _(b):
        at = pl.ds(pl.multiple_of(b * step, step), step)
        total_rows = jnp.zeros((step, slots_n), F32)
        for c in range(chunks):
            total_rows = (total_rows + dot_nt(w1[c, at, :], right[1, c, 0:slots_n, :])
                          + dot_nt(w3[c, at, :], right[2, c, 0:slots_n, :]))
        rows_mine[b] = total_rows.astype(BF)
        rows_swap(b).start()

    for peer in near:
        pl.semaphore_signal(ready, inc=1, device_id=peer, device_id_type=MESH)

    @pl.when(section == 1)
    def _():
        pass_on(0)

    for b in range(width // 128):
        cols = slice(b * 128, (b + 1) * 128)
        s_turned[b // 4, b % 4] = (gate_block * g_rows[:, cols].astype(F32)).T.astype(BF)
    sent += deal(1, s_turned)

    for b in range(blocks):
        rows_swap(b).wait_recv()
        cols = slice(b * step, (b + 1) * step)

        def token_grads(i):
            added = dot_nt(place[i], rows_mine[b]) + dot_nt(place[i], rows_theirs[b])
            grads_both[b, i] = (g_full[i, :, cols].astype(F32) + added).astype(BF)

        token_grads(0)

        @pl.when(section == 1)
        def _():
            token_grads(1)
            hop(b).start()

        in_grad[0, 0, :, cols] = grads_both[b, 0]

    outs = (down_out, gate_out, up_out)
    block = RING * 128

    def left_wait(which):
        for h in range(2):
            for k, step in ((1, step_a), (3, step_b), (2, 2)):
                there = left.at[which, h, :, :, pl.ds(k * 128, 128)]
                remote(there, there, left_send.at[which, h, k - 1], left_recv.at[which, h, k - 1],
                       gather_to[h](step)).wait_recv()

    def multiply(t, h):
        for d in range(2):
            spread_copy(t, h, d, 1 - d).wait_recv()
        for d in range(2):
            pass_copy(t, h, d).wait_recv()
        which = 1 if t == 0 else 0

        @pl.loop(0, half)
        def _(n):
            c = half * h + n
            a = left[which, h].reshape(block, RING * slots_n)
            w1[c, t * block:(t + 1) * block, :] = dot(a, right[t, c]).astype(BF)

    def part_at(t, h, p, row):
        start, count = part_of[p]
        return (pl.ds(half * h + start, count), pl.ds(pl.multiple_of(t * block + row * 128, 128), 128), slice(None))

    def of_block(t, h, p, step):
        return part_at(t, h, p, (reduce_pos[h] + step) % RING)

    def far_sum(t, h, d):
        return remote(w1.at[of_block(t, h, d, 2)], w3.at[part_at(t, h, d, 2)],
                      sum_send.at[t, h, 0, d], sum_recv.at[t, h, 0, d], reduce_to[h](steps[d]))

    def near_sum(t, h, d, p):
        return remote(w1.at[of_block(t, h, p, steps[d])], w3.at[part_at(t, h, p, 1 + 2 * d)],
                      sum_send.at[t, h, 1 + p, d], sum_recv.at[t, h, 1 + p, d], reduce_to[h](steps[d]))

    def reduce_start(t, h):
        copies = [far_sum(t, h, d) for d in range(2)] + [near_sum(t, h, d, 1 - d) for d in range(2)]
        for copy in copies:
            copy.start()
        return copies

    def merge(t, h):
        copies = []
        for d in range(2):
            far_sum(t, h, d).wait_recv()
            here = of_block(t, h, d, steps[d])
            w1[here] = (w1[here].astype(F32) + w3[part_at(t, h, d, 2)].astype(F32)).astype(BF)
            copy = near_sum(t, h, d, d)
            copy.start()
            copies.append(copy)
        return copies

    def total(t, h, c, side):
        here = pl.multiple_of(t * block + reduce_pos[h] * 128 + side * 64, 64)
        value = w1[c, pl.ds(here, 64), :].astype(F32)
        for k in (1, 3):
            there = pl.multiple_of(t * block + k * 128 + side * 64, 64)
            value = value + w3[c, pl.ds(there, 64), :].astype(F32)
        return value

    def x_copy(t, h):
        at = (pl.ds(half * h, half), pl.ds(3 * block + t * 64, 64), slice(None))
        return remote(w1.at[at], w3.at[at], x_send.at[t, h], x_recv.at[t, h], x_peer)

    def reduce_end(t, h):
        for d in range(2):
            for p in range(2):
                near_sum(t, h, d, p).wait_recv()

        @pl.loop(0, half)
        def _(n):
            c = half * h + n
            w1[c, 3 * block + t * 64:3 * block + (t + 1) * 64, :] = total(t, h, c, 1 - x).astype(BF)
        copy = x_copy(t, h)
        copy.start()
        return [copy]

    def finish(t, h):
        x_copy(t, h).wait_recv()
        for n in range(half):
            c = half * h + n
            arrived = w3[c, 3 * block + t * 64:3 * block + (t + 1) * 64, :].astype(F32)
            outs[t][0, :, c * COLS:(c + 1) * COLS] = ((total(t, h, c, x) + arrived) * (1.0 / 32.0)).astype(BF)

    pass_on(1)
    left_wait(1)
    multiply(0, 0)
    pass_on(2)
    multiply(0, 1)
    pl.semaphore_wait(ready, len(near))
    sent += reduce_start(0, 0)
    sent += reduce_start(0, 1)
    left_wait(0)
    for t in (1, 2):
        for h in range(2):
            multiply(t, h)
            sent += reduce_start(t, h)
            sent += merge(t - 1, h)
    for h in range(2):
        sent += reduce_end(0, h)
    for h in range(2):
        sent += merge(2, h)
    for h in range(2):
        sent += reduce_end(1, h)
    value_swap.wait_recv()
    value_out[0] = jnp.sum((value_mine[...] + value_theirs[...]).T, axis=0, keepdims=True)
    for h in range(2):
        finish(0, h)
    for h in range(2):
        sent += reduce_end(2, h)
    for t in (1, 2):
        for h in range(2):
            finish(t, h)

    for copy in sent:
        copy.wait_send()
    for t in range(3):
        for h in range(2):
            for d in range(2):
                pass_copy(t, h, d).wait_send()
    for b in range(blocks):
        rows_swap(b).wait_send()
    value_swap.wait_send()

    @pl.when(section == 0)
    def _():
        x_swap.wait_send()

    @pl.when(section == 1)
    def _():
        for b in range(blocks):
            hop(b).wait_send()


def hand_out(*refs):
    sources, targets, sems = refs[:5], refs[5:10], refs[10]
    copies = [pltpu.make_async_copy(sources[i], targets[i], sems.at[i]) for i in range(5)]
    for copy in copies:
        copy.start()
    for copy in copies:
        copy.wait()


def per_device(layer_inputs, out_grad, w_gate, w_up, w_down, slot_token, slot_gate):
    tok, width = layer_inputs.shape[2:]
    hidden = w_gate.shape[2]
    slots_n = slot_token.shape[2]
    chunks = hidden // COLS
    rows_out = width // (NY * NZ * NX)
    vmem = pl.BlockSpec(memory_space=pltpu.VMEM)
    hbm = pl.BlockSpec(memory_space=pl.ANY)
    sem = pltpu.SemaphoreType.DMA
    grad = jax.ShapeDtypeStruct((1, rows_out, hidden), BF)
    shapes = (
        jax.ShapeDtypeStruct((1, 1, tok, width), BF), grad, grad, grad,
        jax.ShapeDtypeStruct((1, 1, slots_n), F32),
    )
    made = pl.pallas_call(
        body,
        out_shape=shapes,
        in_specs=[vmem, vmem, hbm, hbm, hbm, hbm, hbm],
        out_specs=(vmem,) * 5,
        scratch_shapes=[
            pltpu.VMEM((chunks, width, COLS), BF),
            pltpu.VMEM((chunks, width, COLS), BF),
            pltpu.VMEM((chunks // 2, width, COLS), BF),
            pltpu.VMEM((2, tok, width), BF),
            pltpu.VMEM((2, tok, width), BF),
            pltpu.VMEM((slots_n, width), BF),
            pltpu.VMEM((slots_n, width), BF),
            pltpu.VMEM((RING, RING, 128, slots_n), BF),
            pltpu.VMEM((RING, RING, 128, slots_n), BF),
            pltpu.VMEM((chunks, slots_n, COLS), F32),
            pltpu.VMEM((chunks, slots_n, COLS), F32),
            pltpu.VMEM((3, chunks, RING * slots_n, COLS), BF),
            pltpu.VMEM((2, 2, RING, 128, RING * slots_n), BF),
            pltpu.VMEM((4, width // 4, slots_n), BF),
            pltpu.VMEM((4, width // 4, slots_n), BF),
            pltpu.VMEM((4, 2, tok, width // 4), BF),
            pltpu.VMEM((slots_n, 128), F32),
            pltpu.VMEM((slots_n, 128), F32),
            sem((2, chunks)), sem((chunks // 2,)), sem((2,)),
            sem((3,)), sem((3,)), sem((4,)), sem((4,)), sem((4,)), sem((4,)),
            sem((2, 2, 3)), sem((2, 2, 3)), sem((3, 2, 2, 2)), sem((3, 2, 2, 2)), sem((3, 2, 2)), sem((3, 2, 2)),
            sem((3, 2, 3, 2)), sem((3, 2, 3, 2)), sem((3, 2)), sem((3, 2)),
            pltpu.SemaphoreType.REGULAR, pltpu.SemaphoreType.REGULAR,
        ],
        compiler_params=pltpu.CompilerParams(
            collective_id=0, has_side_effects=True, vmem_limit_bytes=63 * 1024 * 1024),
    )(slot_token, slot_gate, layer_inputs, out_grad, w_gate, w_up, w_down)
    return pl.pallas_call(
        hand_out,
        out_shape=shapes,
        in_specs=[vmem] * 5,
        out_specs=(hbm,) * 5,
        scratch_shapes=[sem((5,))],
    )(*made)


def solution(mesh):
    placed = (
        P("section", None, ("dp", "et"), None),
        P(None, ("dp", "et"), None),
        P("section", None, "et"),
        P("section", None, "et"),
        P("section", None, "et"),
        P("section", None, "dp"),
        P("section", None, "dp"),
    )
    return jax.shard_map(
        per_device,
        mesh=mesh,
        in_specs=placed,
        out_specs=(
            P("section", None, ("dp", "et"), None),
            P("section", "dp", "et"),
            P("section", "dp", "et"),
            P("section", "dp", "et"),
            P("section", None, "dp"),
        ),
        check_vma=False,
    )
```

```python
import jax
import jax.numpy as jnp
from jax import lax
from jax.experimental import pallas as pl
from jax.experimental.pallas import tpu as pltpu
from jax.sharding import PartitionSpec as P

BF = jnp.bfloat16
F32 = jnp.float32
NY, NZ, NX = 4, 4, 2
RING = 4
COLS = 256
W2_RING = 6
MESH = pl.DeviceIdType.MESH


def dot(a, b):
    return jnp.dot(a, b, preferred_element_type=F32)


def dot_nt(a, b):
    return lax.dot_general(a, b, (((1,), (1,)), ((), ())), preferred_element_type=F32)


def body(
    slots_ref, gates_ref, x_hbm, g_hbm, w1_hbm, w3_hbm, w2_hbm,
    in_grad, gate_out, up_out, down_out, value_out,
    w1, w3, w2, x_full, g_full, g_rows, x_group, s_group,
    right, left, rows_mine, rows_theirs, grads_both,
    value_mine, value_theirs,
    load_sem, w2_sem, local_sem, pair_send, pair_recv, rows_send, rows_recv, hop_send, hop_recv,
    group_send, group_recv, far_send, far_recv, sum_send, sum_recv, x_send, x_recv, ready,
):
    section = lax.axis_index("section")
    et = lax.axis_index("et")
    dp = lax.axis_index("dp")
    z, y, x = dp // (NY * NX), (dp // NX) % NY, dp % NX
    slots_n = slots_ref.shape[2]
    tok = x_full.shape[1]
    chunks = w1.shape[0]
    half = chunks // 2
    ring_w2 = w2.shape[0]
    width = w1.shape[1]
    part_of = ((0, (half + 1) // 2), ((half + 1) // 2, half // 2))
    step_a = 1 + 2 * section
    step_b = 3 - 2 * section
    steps = (step_a, step_b)

    def at_y(step):
        return (section, et, z * (NY * NX) + ((y + step) % NY) * NX + x)

    def at_z(step):
        return (section, et, ((z + step) % NZ) * (NY * NX) + y * NX + x)

    pair = (section, 1 - et, dp)
    sibling = (1 - section, et, dp)
    x_peer = (section, et, z * (NY * NX) + y * NX + (1 - x))
    gather_to = (at_y, at_z)
    reduce_to = (at_z, at_y)
    gather_pos = (y, z)
    reduce_pos = (z, y)

    def remote(src, dst, send, recv, device):
        return pltpu.make_async_remote_copy(
            src_ref=src, dst_ref=dst, send_sem=send, recv_sem=recv,
            device_id=device, device_id_type=MESH)

    def w_load(hbm, ref, c, sem):
        start = pl.multiple_of(c * COLS, COLS)
        return pltpu.make_async_copy(hbm.at[0, :, pl.ds(start, COLS)], ref, sem)

    x_load = pltpu.make_async_copy(x_hbm.at[0, 0], x_full.at[0], local_sem.at[0])
    g_load = pltpu.make_async_copy(g_hbm.at[0], g_full.at[0], local_sem.at[1])
    x_load.start()

    @pl.when(section == 1)
    def _():
        g_load.start()

    @pl.loop(0, chunks)
    def _(c):
        w_load(w1_hbm, w1.at[c], c, load_sem.at[0, c]).start()
        w_load(w3_hbm, w3.at[c], c, load_sem.at[1, c]).start()

    @pl.loop(0, ring_w2)
    def _(c):
        w_load(w2_hbm, w2.at[c], c, w2_sem.at[c]).start()

    barrier = pltpu.get_barrier_semaphore()
    near = [x_peer] + [at_y(k) for k in (1, 3)] + [at_z(k) for k in (1, 3)]
    peers = [pair, sibling] + near
    for peer in peers:
        pl.semaphore_signal(barrier, inc=1, device_id=peer, device_id_type=MESH)
    pl.semaphore_wait(barrier, len(peers))

    x_swap = remote(x_hbm.at[0, 0], x_full.at[1], pair_send.at[0], pair_recv.at[0], pair)
    g_swap = remote(g_hbm.at[0], g_full.at[1], pair_send.at[1], pair_recv.at[1], pair)

    x_swap.start()

    @pl.when(section == 1)
    def _():
        x_swap.wait_send()
        g_swap.start()

    def down_rows(row):
        return jnp.broadcast_to(row.astype(F32), (slots_n, slots_n)).T

    offsets = (et * tok, (1 - et) * tok)
    slot_rows = down_rows(slots_ref[0]).astype(jnp.int32)
    across = lax.broadcasted_iota(jnp.int32, (slots_n, tok), 1)
    pick = [jnp.where(slot_rows == across + o, 1.0, 0.0).astype(BF) for o in offsets]
    along = lax.broadcasted_iota(jnp.int32, (tok, slots_n), 0)
    place = [jnp.where(slots_ref[0] == along + o, 1.0, 0.0).astype(BF) for o in offsets]

    groups = (x_group, s_group)
    span = width // 2

    def piece(which, h, p, k):
        return groups[which].at[h, pl.ds(k * slots_n, slots_n), pl.ds(p * span, span)]

    def spread_copy(which, h, d, p):
        return remote(piece(which, h, p, 0), piece(which, h, p, 1 + 2 * d),
                      group_send.at[which, h, d, p], group_recv.at[which, h, d, p], gather_to[h](steps[d]))

    def pass_copy(which, h, d):
        return remote(piece(which, h, d, 1 + 2 * d), piece(which, h, d, 2),
                      far_send.at[which, h, d], far_recv.at[which, h, d], gather_to[h](steps[d]))

    def spread(which):
        copies = []
        for d, p in ((0, 0), (1, 1), (0, 1), (1, 0)):
            for h in range(2):
                copy = spread_copy(which, h, d, p)
                copy.start()
                copies.append(copy)
        return copies

    def pass_on(which):
        for h in range(2):
            for d in range(2):
                spread_copy(which, h, d, d).wait_recv()
                pass_copy(which, h, d).start()

    def group_wait(which):
        for h in range(2):
            for d in range(2):
                spread_copy(which, h, d, 1 - d).wait_recv()
                pass_copy(which, h, d).wait_recv()

    own = pl.ds(0, slots_n)
    others = pl.ds(slots_n, (RING - 1) * slots_n)

    def forward(c, rows, at):
        pre_gate = dot(rows, w1[c])
        pre_up = dot(rows, w3[c])
        sigma = jax.nn.sigmoid(pre_gate)
        active = pre_gate * sigma
        right[0, c, at, :] = (active * pre_up).astype(BF)
        right[1, c, at, :] = (pre_up * sigma * (1.0 + pre_gate * (1.0 - sigma))).astype(BF)
        right[2, c, at, :] = active.astype(BF)

    def forward_others():
        group_wait(0)

        @pl.loop(0, chunks)
        def _(c):
            forward(c, x_group[c // half, others, :], others)

    def backward(c, scaled, at):
        for t in (1, 2):
            right[t, c, at, :] = (scaled * right[t, c, at, :].astype(F32)).astype(BF)

    def w2_load(i):
        return w_load(w2_hbm, w2.at[i % ring_w2], i % chunks, w2_sem.at[i % ring_w2])

    def w2_next(i):
        @pl.when(i + ring_w2 < 2 * chunks)
        def _():
            w2_load(i + ring_w2).start()

    x_load.wait()
    x_swap.wait_recv()
    picked = (dot(pick[0], x_full[0]) + dot(pick[1], x_full[1])).astype(BF)
    for h in range(2):
        x_group[h, own, :] = picked
    sent = spread(0)

    @pl.loop(0, chunks)
    def _(c):
        w_load(w1_hbm, w1.at[c], c, load_sem.at[0, c]).wait()
        w_load(w3_hbm, w3.at[c], c, load_sem.at[1, c]).wait()
        forward(c, x_group[0, own, :], own)

    pass_on(0)

    blocks = grads_both.shape[0]
    step = width // blocks

    def hop(b):
        return remote(grads_both.at[b], g_full.at[:, :, pl.ds(b * step, step)],
                      hop_send.at[b], hop_recv.at[b], sibling)

    @pl.when(section == 1)
    def _():
        g_load.wait()
        g_swap.wait_recv()

    @pl.when(section == 0)
    def _():
        forward_others()

    gate_block = down_rows(gates_ref[0])
    gates = jnp.concatenate([gate_block] * (COLS // 128), axis=1)
    for b in range(blocks):
        cols = slice(b * step, (b + 1) * step)

        @pl.when(section == 0)
        def _():
            hop(b).wait_recv()

        rows = (dot(pick[0], g_full[0, :, cols]) + dot(pick[1], g_full[1, :, cols])).astype(BF)
        g_rows[:, cols] = rows
        scaled_rows = (jnp.concatenate([gate_block] * (step // 128), axis=1) * rows.astype(F32)).astype(BF)
        for h in range(2):
            s_group[h, own, cols] = scaled_rows

    sent += spread(1)
    value_mine[...] = jnp.zeros_like(value_mine)

    @pl.loop(0, chunks)
    def _(c):
        w2_load(c).wait()
        back = dot(g_rows[...], w2[c % ring_w2])
        w2_next(c)
        product = right[0, c, own, :].astype(F32) * back
        value_mine[...] += product[:, :128] + product[:, 128:]
        backward(c, gates * back, own)

    value_swap = remote(value_mine, value_theirs, pair_send.at[2], pair_recv.at[2], pair)
    value_swap.start()

    def rows_swap(b):
        return remote(rows_mine.at[b], rows_theirs.at[b], rows_send.at[b], rows_recv.at[b], pair)

    @pl.loop(0, blocks)
    def _(b):
        at = pl.ds(pl.multiple_of(b * step, step), step)
        total_rows = jnp.zeros((step, slots_n), F32)
        for c in range(chunks):
            total_rows = (total_rows + dot_nt(w1[c, at, :], right[1, c, own, :])
                          + dot_nt(w3[c, at, :], right[2, c, own, :]))
        rows_mine[b] = total_rows.astype(BF)
        rows_swap(b).start()

    pass_on(1)

    for b in range(blocks):
        rows_swap(b).wait_recv()
        cols = slice(b * step, (b + 1) * step)

        def token_grads(i):
            added = dot_nt(place[i], rows_mine[b]) + dot_nt(place[i], rows_theirs[b])
            grads_both[b, i] = (g_full[i, :, cols].astype(F32) + added).astype(BF)

        token_grads(0)

        @pl.when(section == 1)
        def _():
            token_grads(1)
            hop(b).start()

        in_grad[0, 0, :, cols] = grads_both[b, 0]

    outs = (down_out, gate_out, up_out)
    block = RING * 128

    def left_make(which):
        for h in range(2):
            for j in range(RING):
                at = (j * RING + gather_pos[h]) if h == 0 else (gather_pos[h] * RING + j)
                cols = pl.ds(pl.multiple_of(at * 128, 128), 128)
                for k in range(RING):
                    tile = groups[which][h, k * slots_n:(k + 1) * slots_n, cols].astype(F32)
                    left[which, h, j * 128:(j + 1) * 128, k * slots_n:(k + 1) * slots_n] = tile.T.astype(BF)

    def multiply(t, h):
        which = 1 if t == 0 else 0

        @pl.loop(0, half)
        def _(n):
            c = half * h + n
            w1[c, t * block:(t + 1) * block, :] = dot(left[which, h], right[t, c]).astype(BF)

    def part_at(t, h, p, row):
        start, count = part_of[p]
        return (pl.ds(half * h + start, count), pl.ds(pl.multiple_of(t * block + row * 128, 128), 128), slice(None))

    def of_block(t, h, p, step):
        return part_at(t, h, p, (reduce_pos[h] + step) % RING)

    def far_sum(t, h, d):
        return remote(w1.at[of_block(t, h, d, 2)], w3.at[part_at(t, h, d, 2)],
                      sum_send.at[t, h, 0, d], sum_recv.at[t, h, 0, d], reduce_to[h](steps[d]))

    def near_sum(t, h, d, p):
        return remote(w1.at[of_block(t, h, p, steps[d])], w3.at[part_at(t, h, p, 1 + 2 * d)],
                      sum_send.at[t, h, 1 + p, d], sum_recv.at[t, h, 1 + p, d], reduce_to[h](steps[d]))

    def reduce_start(t, h):
        copies = [far_sum(t, h, d) for d in range(2)] + [near_sum(t, h, d, 1 - d) for d in range(2)]
        for copy in copies:
            copy.start()
        return copies

    def merge(t, h):
        copies = []
        for d in range(2):
            far_sum(t, h, d).wait_recv()
            here = of_block(t, h, d, steps[d])
            w1[here] = (w1[here].astype(F32) + w3[part_at(t, h, d, 2)].astype(F32)).astype(BF)
            copy = near_sum(t, h, d, d)
            copy.start()
            copies.append(copy)
        return copies

    def total(t, h, c, side):
        here = pl.multiple_of(t * block + reduce_pos[h] * 128 + side * 64, 64)
        value = w1[c, pl.ds(here, 64), :].astype(F32)
        for k in (1, 3):
            there = pl.multiple_of(t * block + k * 128 + side * 64, 64)
            value = value + w3[c, pl.ds(there, 64), :].astype(F32)
        return value

    def x_copy(t, h):
        at = (pl.ds(half * h, half), pl.ds(3 * block + t * 64, 64), slice(None))
        return remote(w1.at[at], w3.at[at], x_send.at[t, h], x_recv.at[t, h], x_peer)

    def reduce_end(t, h):
        for d in range(2):
            for p in range(2):
                near_sum(t, h, d, p).wait_recv()

        @pl.loop(0, half)
        def _(n):
            c = half * h + n
            w1[c, 3 * block + t * 64:3 * block + (t + 1) * 64, :] = total(t, h, c, 1 - x).astype(BF)
        copy = x_copy(t, h)
        copy.start()
        return [copy]

    def finish(t, h):
        x_copy(t, h).wait_recv()
        for n in range(half):
            c = half * h + n
            arrived = w3[c, 3 * block + t * 64:3 * block + (t + 1) * 64, :].astype(F32)
            outs[t][0, :, c * COLS:(c + 1) * COLS] = ((total(t, h, c, x) + arrived) * (1.0 / 32.0)).astype(BF)

    @pl.when(section == 1)
    def _():
        forward_others()

    for peer in near:
        pl.semaphore_signal(ready, inc=1, device_id=peer, device_id_type=MESH)
    group_wait(1)
    left_make(1)
    multiply(0, 0)
    pl.semaphore_wait(ready, len(near))
    sent += reduce_start(0, 0)
    multiply(0, 1)
    sent += reduce_start(0, 1)

    @pl.loop(0, chunks)
    def _(c):
        i = chunks + c
        w2_load(i).wait()
        scaled = dot(s_group[c // half, others, :], w2[i % ring_w2])
        w2_next(i)
        backward(c, scaled, others)

    left_make(0)
    for t in (1, 2):
        for h in range(2):
            multiply(t, h)
            sent += reduce_start(t, h)
            sent += merge(t - 1, h)
    for h in range(2):
        sent += reduce_end(0, h)
    for h in range(2):
        sent += merge(2, h)
    for h in range(2):
        sent += reduce_end(1, h)
    value_swap.wait_recv()
    value_out[0] = jnp.sum((value_mine[...] + value_theirs[...]).T, axis=0, keepdims=True)
    for h in range(2):
        finish(0, h)
    for h in range(2):
        sent += reduce_end(2, h)
    for t in (1, 2):
        for h in range(2):
            finish(t, h)

    for copy in sent:
        copy.wait_send()
    for which in range(2):
        for h in range(2):
            for d in range(2):
                pass_copy(which, h, d).wait_send()
    for b in range(blocks):
        rows_swap(b).wait_send()
    value_swap.wait_send()

    @pl.when(section == 0)
    def _():
        x_swap.wait_send()

    @pl.when(section == 1)
    def _():
        g_swap.wait_send()
        for b in range(blocks):
            hop(b).wait_send()


def hand_out(*refs):
    sources, targets, sems = refs[:5], refs[5:10], refs[10]
    copies = [pltpu.make_async_copy(sources[i], targets[i], sems.at[i]) for i in range(5)]
    for copy in copies:
        copy.start()
    for copy in copies:
        copy.wait()


def per_device(layer_inputs, out_grad, w_gate, w_up, w_down, slot_token, slot_gate):
    tok, width = layer_inputs.shape[2:]
    hidden = w_gate.shape[2]
    slots_n = slot_token.shape[2]
    chunks = hidden // COLS
    rows_out = width // (NY * NZ * NX)
    vmem = pl.BlockSpec(memory_space=pltpu.VMEM)
    hbm = pl.BlockSpec(memory_space=pl.ANY)
    sem = pltpu.SemaphoreType.DMA
    grad = jax.ShapeDtypeStruct((1, rows_out, hidden), BF)
    shapes = (
        jax.ShapeDtypeStruct((1, 1, tok, width), BF), grad, grad, grad,
        jax.ShapeDtypeStruct((1, 1, slots_n), F32),
    )
    made = pl.pallas_call(
        body,
        out_shape=shapes,
        in_specs=[vmem, vmem, hbm, hbm, hbm, hbm, hbm],
        out_specs=(vmem,) * 5,
        scratch_shapes=[
            pltpu.VMEM((chunks, width, COLS), BF),
            pltpu.VMEM((chunks, width, COLS), BF),
            pltpu.VMEM((W2_RING, width, COLS), BF),
            pltpu.VMEM((2, tok, width), BF),
            pltpu.VMEM((2, tok, width), BF),
            pltpu.VMEM((slots_n, width), BF),
            pltpu.VMEM((2, RING * slots_n, width), BF),
            pltpu.VMEM((2, RING * slots_n, width), BF),
            pltpu.VMEM((3, chunks, RING * slots_n, COLS), BF),
            pltpu.VMEM((2, 2, RING * 128, RING * slots_n), BF),
            pltpu.VMEM((4, width // 4, slots_n), BF),
            pltpu.VMEM((4, width // 4, slots_n), BF),
            pltpu.VMEM((4, 2, tok, width // 4), BF),
            pltpu.VMEM((slots_n, 128), F32),
            pltpu.VMEM((slots_n, 128), F32),
            sem((2, chunks)), sem((W2_RING,)), sem((2,)),
            sem((3,)), sem((3,)), sem((4,)), sem((4,)), sem((4,)), sem((4,)),
            sem((2, 2, 2, 2)), sem((2, 2, 2, 2)), sem((2, 2, 2)), sem((2, 2, 2)),
            sem((3, 2, 3, 2)), sem((3, 2, 3, 2)), sem((3, 2)), sem((3, 2)),
            pltpu.SemaphoreType.REGULAR,
        ],
        compiler_params=pltpu.CompilerParams(
            collective_id=0, has_side_effects=True, vmem_limit_bytes=63 * 1024 * 1024),
    )(slot_token, slot_gate, layer_inputs, out_grad, w_gate, w_up, w_down)
    return pl.pallas_call(
        hand_out,
        out_shape=shapes,
        in_specs=[vmem] * 5,
        out_specs=(hbm,) * 5,
        scratch_shapes=[sem((5,))],
    )(*made)


def solution(mesh):
    placed = (
        P("section", None, ("dp", "et"), None),
        P(None, ("dp", "et"), None),
        P("section", None, "et"),
        P("section", None, "et"),
        P("section", None, "et"),
        P("section", None, "dp"),
        P("section", None, "dp"),
    )
    return jax.shard_map(
        per_device,
        mesh=mesh,
        in_specs=placed,
        out_specs=(
            P("section", None, ("dp", "et"), None),
            P("section", "dp", "et"),
            P("section", "dp", "et"),
            P("section", "dp", "et"),
            P("section", None, "dp"),
        ),
        check_vma=False,
    )
```

```python
import jax
import jax.numpy as jnp
from jax import lax
from jax.experimental import pallas as pl
from jax.experimental.pallas import tpu as pltpu
from jax.sharding import PartitionSpec as P

BF = jnp.bfloat16
F32 = jnp.float32
NY, NZ, NX = 4, 4, 2
RING = 4
COLS = 256
W2_RING = 5
MESH = pl.DeviceIdType.MESH


def dot(a, b):
    return jnp.dot(a, b, preferred_element_type=F32)


def dot_nt(a, b):
    return lax.dot_general(a, b, (((1,), (1,)), ((), ())), preferred_element_type=F32)


def body(
    slots_ref, gates_ref, x_hbm, g_hbm, w1_hbm, w3_hbm, w2_hbm,
    in_grad, gate_out, up_out, down_out, value_out,
    w1, w3, w2, x_full, g_full, g_rows, x_group, s_group,
    x_turned, s_turned, right, left, rows_mine, rows_theirs, grads_both,
    value_mine, value_theirs,
    load_sem, w2_sem, local_sem, pair_send, pair_recv, rows_send, rows_recv, hop_send, hop_recv,
    left_send, left_recv, right_send, right_recv, pass_send, pass_recv,
    group_send, group_recv, far_send, far_recv, sum_send, sum_recv, x_send, x_recv, first_send, first_recv, ready,
):
    section = lax.axis_index("section")
    et = lax.axis_index("et")
    dp = lax.axis_index("dp")
    z, y, x = dp // (NY * NX), (dp // NX) % NY, dp % NX
    slots_n = slots_ref.shape[2]
    tok = x_full.shape[1]
    chunks = w1.shape[0]
    half = chunks // 2
    ring_w2 = w2.shape[0]
    width = w1.shape[1]
    part_of = ((0, (half + 1) // 2), ((half + 1) // 2, half // 2))
    step_a = 1 + 2 * section
    step_b = 3 - 2 * section
    steps = (step_a, step_b)

    def at_y(step):
        return (section, et, z * (NY * NX) + ((y + step) % NY) * NX + x)

    def at_z(step):
        return (section, et, ((z + step) % NZ) * (NY * NX) + y * NX + x)

    pair = (section, 1 - et, dp)
    sibling = (1 - section, et, dp)
    x_peer = (section, et, z * (NY * NX) + y * NX + (1 - x))
    gather_to = (at_y, at_z)
    reduce_to = (at_z, at_y)
    gather_pos = (y, z)
    reduce_pos = (z, y)

    def remote(src, dst, send, recv, device):
        return pltpu.make_async_remote_copy(
            src_ref=src, dst_ref=dst, send_sem=send, recv_sem=recv,
            device_id=device, device_id_type=MESH)

    def w_load(hbm, ref, c, sem):
        start = pl.multiple_of(c * COLS, COLS)
        return pltpu.make_async_copy(hbm.at[0, :, pl.ds(start, COLS)], ref, sem)

    x_load = pltpu.make_async_copy(x_hbm.at[0, 0], x_full.at[0], local_sem.at[0])
    g_load = pltpu.make_async_copy(g_hbm.at[0], g_full.at[0], local_sem.at[1])
    x_load.start()

    @pl.when(section == 1)
    def _():
        g_load.start()

    @pl.loop(0, chunks)
    def _(c):
        w_load(w1_hbm, w1.at[c], c, load_sem.at[0, c]).start()
        w_load(w3_hbm, w3.at[c], c, load_sem.at[1, c]).start()

    @pl.loop(0, ring_w2)
    def _(c):
        w_load(w2_hbm, w2.at[c], c, w2_sem.at[c]).start()

    barrier = pltpu.get_barrier_semaphore()
    near = [x_peer] + [at_y(k) for k in (1, 3)] + [at_z(k) for k in (1, 3)]
    peers = [pair, sibling, at_y(2), at_z(2)] + near
    for peer in peers:
        pl.semaphore_signal(barrier, inc=1, device_id=peer, device_id_type=MESH)
    pl.semaphore_wait(barrier, len(peers))

    x_swap = remote(x_hbm.at[0, 0], x_full.at[1], pair_send.at[0], pair_recv.at[0], pair)
    g_swap = remote(g_hbm.at[0], g_full.at[1], pair_send.at[1], pair_recv.at[1], pair)

    x_swap.start()

    @pl.when(section == 1)
    def _():
        x_swap.wait_send()
        g_swap.start()

    def down_rows(row):
        return jnp.broadcast_to(row.astype(F32), (slots_n, slots_n)).T

    offsets = (et * tok, (1 - et) * tok)
    slot_rows = down_rows(slots_ref[0]).astype(jnp.int32)
    across = lax.broadcasted_iota(jnp.int32, (slots_n, tok), 1)
    pick = [jnp.where(slot_rows == across + o, 1.0, 0.0).astype(BF) for o in offsets]
    along = lax.broadcasted_iota(jnp.int32, (tok, slots_n), 0)
    place = [jnp.where(slots_ref[0] == along + o, 1.0, 0.0).astype(BF) for o in offsets]

    def turn(rows, into):
        for b in range(width // 128):
            block = rows[:, b * 128:(b + 1) * 128].astype(F32)
            into[b // 4, b % 4] = block.T.astype(BF)

    def deal_copies(which):
        source = (x_turned, s_turned)[which]
        copies = []
        for h in range(2):
            for k, step in ((2, 2), (1, step_a), (3, step_b)):
                there = (gather_pos[h] + step) % RING
                share = source.at[:, there] if h == 0 else source.at[there]
                copies.append(remote(share, left.at[which, h, :, :, pl.ds(k * 128, 128)],
                                     left_send.at[which, h, k - 1], left_recv.at[which, h, k - 1],
                                     gather_to[h](step)))
        return copies

    def deal(which):
        source = (x_turned, s_turned)[which]
        left[which, 0, :, :, 0:128] = source[:, gather_pos[0]]
        left[which, 1, :, :, 0:128] = source[gather_pos[1]]
        for copy in deal_copies(which):
            copy.start()

    def right_piece(t, h, p, k):
        start, count = part_of[p]
        return right.at[t, pl.ds(half * h + start, count), pl.ds(k * slots_n, slots_n), :]

    def right_copy(t, h, d, p):
        return remote(right_piece(t, h, p, 0), right_piece(t, h, p, 1 + 2 * d),
                      right_send.at[t, h, d, p], right_recv.at[t, h, d, p], gather_to[h](steps[d]))

    def right_pass(t, h, d):
        return remote(right_piece(t, h, d, 1 + 2 * d), right_piece(t, h, d, 2),
                      pass_send.at[t, h, d], pass_recv.at[t, h, d], gather_to[h](steps[d]))

    def right_spread(t):
        for d, p in ((0, 0), (1, 1), (0, 1), (1, 0)):
            for h in range(2):
                right_copy(t, h, d, p).start()

    def right_pass_on(t):
        for h in range(2):
            for d in range(2):
                right_copy(t, h, d, d).wait_recv()
                right_pass(t, h, d).start()

    def right_wait(t):
        for h in range(2):
            for d in range(2):
                right_copy(t, h, d, 1 - d).wait_recv()
                right_pass(t, h, d).wait_recv()

    groups = (x_group, s_group)
    span = width // 2

    def piece(which, h, p, k):
        return groups[which].at[h, pl.ds(k * slots_n, slots_n), pl.ds(p * span, span)]

    def spread_copy(which, h, d, p):
        return remote(piece(which, h, p, 0), piece(which, h, p, 1 + 2 * d),
                      group_send.at[which, h, d, p], group_recv.at[which, h, d, p], gather_to[h](steps[d]))

    def pass_copy(which, h, d):
        return remote(piece(which, h, d, 1 + 2 * d), piece(which, h, d, 2),
                      far_send.at[which, h, d], far_recv.at[which, h, d], gather_to[h](steps[d]))

    def spread(which):
        for d, p in ((0, 0), (1, 1), (0, 1), (1, 0)):
            for h in range(2):
                spread_copy(which, h, d, p).start()

    def pass_on(which):
        for h in range(2):
            for d in range(2):
                spread_copy(which, h, d, d).wait_recv()
                pass_copy(which, h, d).start()

    def group_wait(which):
        for h in range(2):
            for d in range(2):
                spread_copy(which, h, d, 1 - d).wait_recv()
                pass_copy(which, h, d).wait_recv()

    def left_make(which):
        for h in range(2):
            for j in range(RING):
                at = (j * RING + gather_pos[h]) if h == 0 else (gather_pos[h] * RING + j)
                cols = pl.ds(pl.multiple_of(at * 128, 128), 128)
                for k in range(RING):
                    tile = groups[which][h, k * slots_n:(k + 1) * slots_n, cols].astype(F32)
                    left[which, h, j, :, k * slots_n:(k + 1) * slots_n] = tile.T.astype(BF)

    own = pl.ds(0, slots_n)
    others = pl.ds(slots_n, (RING - 1) * slots_n)

    def forward(c, rows, at):
        pre_gate = dot(rows, w1[c])
        pre_up = dot(rows, w3[c])
        sigma = jax.nn.sigmoid(pre_gate)
        active = pre_gate * sigma
        right[0, c, at, :] = (active * pre_up).astype(BF)
        right[1, c, at, :] = (pre_up * sigma * (1.0 + pre_gate * (1.0 - sigma))).astype(BF)
        right[2, c, at, :] = active.astype(BF)

    def forward_others():
        group_wait(0)

        @pl.loop(0, chunks)
        def _(c):
            forward(c, x_group[c // half, others, :], others)

    def backward(c, scaled, at):
        for t in (1, 2):
            right[t, c, at, :] = (scaled * right[t, c, at, :].astype(F32)).astype(BF)

    def w2_load(i):
        return w_load(w2_hbm, w2.at[i % ring_w2], i % chunks, w2_sem.at[i % ring_w2])

    def w2_next(i):
        @pl.when(i + ring_w2 < (2 - section) * chunks)
        def _():
            w2_load(i + ring_w2).start()

    x_load.wait()
    x_swap.wait_recv()
    picked = (dot(pick[0], x_full[0]) + dot(pick[1], x_full[1])).astype(BF)
    for h in range(2):
        x_group[h, own, :] = picked
    @pl.when(section == 0)
    def _():
        spread(0)

    @pl.when(section == 1)
    def _():
        turn(x_group.at[0, own], x_turned)

    @pl.loop(0, chunks)
    def _(c):
        w_load(w1_hbm, w1.at[c], c, load_sem.at[0, c]).wait()
        w_load(w3_hbm, w3.at[c], c, load_sem.at[1, c]).wait()
        forward(c, x_group[0, own, :], own)

    blocks = grads_both.shape[0]
    step = width // blocks

    def hop(b):
        return remote(grads_both.at[b], g_full.at[:, :, pl.ds(b * step, step)],
                      hop_send.at[b], hop_recv.at[b], sibling)

    @pl.when(section == 1)
    def _():
        right_spread(0)
        g_load.wait()
        g_swap.wait_recv()

    @pl.when(section == 0)
    def _():
        pass_on(0)
        forward_others()
        left_make(0)

    gate_block = down_rows(gates_ref[0])
    gates = jnp.concatenate([gate_block] * (COLS // 128), axis=1)
    for b in range(blocks):
        cols = slice(b * step, (b + 1) * step)

        @pl.when(section == 0)
        def _():
            hop(b).wait_recv()

        rows = (dot(pick[0], g_full[0, :, cols]) + dot(pick[1], g_full[1, :, cols])).astype(BF)
        g_rows[:, cols] = rows
        scaled_rows = (jnp.concatenate([gate_block] * (step // 128), axis=1) * rows.astype(F32)).astype(BF)
        for h in range(2):
            s_group[h, own, cols] = scaled_rows

    @pl.when(section == 0)
    def _():
        spread(1)

    value_mine[...] = jnp.zeros_like(value_mine)

    @pl.loop(0, chunks)
    def _(c):
        w2_load(c).wait()
        back = dot(g_rows[...], w2[c % ring_w2])
        w2_next(c)
        product = right[0, c, own, :].astype(F32) * back
        value_mine[...] += product[:, :128] + product[:, 128:]
        backward(c, gates * back, own)

    @pl.when(section == 1)
    def _():
        right_spread(1)
        right_spread(2)

    value_swap = remote(value_mine, value_theirs, pair_send.at[2], pair_recv.at[2], pair)
    value_swap.start()

    def rows_swap(b):
        return remote(rows_mine.at[b], rows_theirs.at[b], rows_send.at[b], rows_recv.at[b], pair)

    @pl.loop(0, blocks)
    def _(b):
        at = pl.ds(pl.multiple_of(b * step, step), step)
        total_rows = jnp.zeros((step, slots_n), F32)
        for c in range(chunks):
            total_rows = (total_rows + dot_nt(w1[c, at, :], right[1, c, own, :])
                          + dot_nt(w3[c, at, :], right[2, c, own, :]))
        rows_mine[b] = total_rows.astype(BF)
        rows_swap(b).start()

        @pl.when((section == 0) & (b == 1))
        def _():
            pass_on(1)

    @pl.when(section == 1)
    def _():
        right_pass_on(0)
        turn(s_group.at[0, own], s_turned)
        deal(1)
        deal(0)

    def token_grads(b, halves):
        rows_swap(b).wait_recv()
        cols = slice(b * step, (b + 1) * step)
        for i in halves:
            added = dot_nt(place[i], rows_mine[b]) + dot_nt(place[i], rows_theirs[b])
            grads_both[b, i] = (g_full[i, :, cols].astype(F32) + added).astype(BF)
        in_grad[0, 0, :, cols] = grads_both[b, 0]

    @pl.when(section == 1)
    def _():
        for b in range(blocks):
            token_grads(b, (0, 1))
            hop(b).start()

    outs = (down_out, gate_out, up_out)
    block = RING * 128

    def multiply(t, h):
        which = 1 if t == 0 else 0

        @pl.loop(0, half)
        def _(n):
            c = half * h + n
            w1[c, t * block:(t + 1) * block, :] = dot(left[which, h].reshape(block, RING * slots_n), right[t, c]).astype(BF)

    def rows_at(t, row, side, early):
        count = 64 if early else 128
        at = t * block + row * 128 + (side * 64 if early else 0)
        return pl.ds(pl.multiple_of(at, 64), count)

    def part_at(t, h, p, row, early):
        start, count = part_of[p]
        return (pl.ds(half * h + start, count), rows_at(t, row, 0, early), slice(None))

    def of_block(t, h, p, step, early):
        start, count = part_of[p]
        return (pl.ds(half * h + start, count), rows_at(t, (reduce_pos[h] + step) % RING, x, early), slice(None))

    def first_sum(h, j):
        cols = pl.ds(half * h, half)
        return remote(w1.at[cols, pl.ds(pl.multiple_of(j * 128 + (1 - x) * 64, 64), 64), :],
                      w3.at[cols, pl.ds(j * 128 + 64, 64), :], first_send.at[h, j], first_recv.at[h, j], x_peer)

    def first_start(h):
        for j in range(RING):
            first_sum(h, j).start()

    def first_end(h):
        for j in range(RING):
            first_sum(h, j).wait_recv()
            cols = pl.ds(half * h, half)
            mine = (cols, pl.ds(pl.multiple_of(j * 128 + x * 64, 64), 64), slice(None))
            theirs = (cols, pl.ds(j * 128 + 64, 64), slice(None))
            w1[mine] = (w1[mine].astype(F32) + w3[theirs].astype(F32)).astype(BF)

    def far_sum(t, h, d, early):
        return remote(w1.at[of_block(t, h, d, 2, early)], w3.at[part_at(t, h, d, 2, early)],
                      sum_send.at[t, h, 0, d], sum_recv.at[t, h, 0, d], reduce_to[h](steps[d]))

    def near_sum(t, h, d, p, early):
        return remote(w1.at[of_block(t, h, p, steps[d], early)], w3.at[part_at(t, h, p, 1 + 2 * d, early)],
                      sum_send.at[t, h, 1 + p, d], sum_recv.at[t, h, 1 + p, d], reduce_to[h](steps[d]))

    def reduce_start(t, h, early=False):
        for d in range(2):
            far_sum(t, h, d, early).start()
        for d in range(2):
            near_sum(t, h, d, 1 - d, early).start()

    def merge(t, h, early=False):
        for d in range(2):
            far_sum(t, h, d, early).wait_recv()
            here = of_block(t, h, d, steps[d], early)
            w1[here] = (w1[here].astype(F32) + w3[part_at(t, h, d, 2, early)].astype(F32)).astype(BF)
            near_sum(t, h, d, d, early).start()

    def reduce_sent(t, h, early=False):
        for d in range(2):
            far_sum(t, h, d, early).wait_send()
            for p in range(2):
                near_sum(t, h, d, p, early).wait_send()
            if not early:
                x_copy(t, h, d).wait_send()

    def total(t, h, c, side, early):
        here = pl.multiple_of(t * block + reduce_pos[h] * 128 + side * 64, 64)
        value = w1[c, pl.ds(here, 64), :].astype(F32)
        for k in (1, 3):
            there = pl.multiple_of(t * block + k * 128 + (0 if early else side * 64), 64)
            value = value + w3[c, pl.ds(there, 64), :].astype(F32)
        return value

    def x_copy(t, h, p):
        start, count = part_of[p]
        at = (pl.ds(half * h + start, count), pl.ds(3 * block + t * 64, 64), slice(None))
        return remote(w1.at[at], w3.at[at], x_send.at[t, h, p], x_recv.at[t, h, p], x_peer)

    def near_wait(t, h, p, early):
        for d in range(2):
            near_sum(t, h, d, p, early).wait_recv()

    def reduce_end(t, h):
        for p in range(2):
            near_wait(t, h, p, False)
            start, count = part_of[p]

            @pl.loop(0, count)
            def _(n):
                c = half * h + start + n
                w1[c, 3 * block + t * 64:3 * block + (t + 1) * 64, :] = total(t, h, c, 1 - x, False).astype(BF)
            x_copy(t, h, p).start()

    def finish(t, h, early=False):
        for p in range(2):
            if early:
                near_wait(t, h, p, True)
            else:
                x_copy(t, h, p).wait_recv()
            start, count = part_of[p]
            for n in range(start, start + count):
                c = half * h + n
                value = total(t, h, c, x, early)
                if not early:
                    value = value + w3[c, 3 * block + t * 64:3 * block + (t + 1) * 64, :].astype(F32)
                outs[t][0, :, c * COLS:(c + 1) * COLS] = (value * (1.0 / 32.0)).astype(BF)

    for peer in near:
        pl.semaphore_signal(ready, inc=1, device_id=peer, device_id_type=MESH)

    @pl.when(section == 0)
    def _():
        group_wait(1)
        left_make(1)

    @pl.when(section == 1)
    def _():
        right_pass_on(1)
        for copy in deal_copies(1):
            copy.wait_recv()
        right_wait(0)

    multiply(0, 0)
    pl.semaphore_wait(ready, len(near))

    @pl.when(section == 0)
    def _():
        reduce_start(0, 0)

    @pl.when(section == 1)
    def _():
        first_start(0)
        right_pass_on(2)

    multiply(0, 1)

    @pl.when(section == 0)
    def _():
        reduce_start(0, 1)

        @pl.loop(0, chunks)
        def _(c):
            i = chunks + c
            w2_load(i).wait()
            scaled = dot(s_group[c // half, others, :], w2[i % ring_w2])
            w2_next(i)
            backward(c, scaled, others)

    @pl.when(section == 1)
    def _():
        first_start(1)
        for copy in deal_copies(0):
            copy.wait_recv()
        right_wait(1)

    multiply(1, 0)
    reduce_start(1, 0)

    @pl.when(section == 0)
    def _():
        merge(0, 0)

    multiply(1, 1)
    reduce_start(1, 1)

    @pl.when(section == 0)
    def _():
        merge(0, 1)

    @pl.when(section == 1)
    def _():
        right_wait(2)

    for h in range(2):
        multiply(2, h)
        reduce_start(2, h)
        merge(1, h)

    @pl.when(section == 0)
    def _():
        for h in range(2):
            reduce_end(0, h)
        for b in range(blocks):
            token_grads(b, (0,))

    for h in range(2):
        merge(2, h)

    @pl.when(section == 1)
    def _():
        for h in range(2):
            first_end(h)
            reduce_start(0, h, True)

    for h in range(2):
        reduce_end(1, h)

    @pl.when(section == 1)
    def _():
        for h in range(2):
            merge(0, h, True)

    value_swap.wait_recv()
    value_out[0] = jnp.sum((value_mine[...] + value_theirs[...]).T, axis=0, keepdims=True)

    @pl.when(section == 0)
    def _():
        for h in range(2):
            finish(0, h)

    for h in range(2):
        reduce_end(2, h)

    @pl.when(section == 1)
    def _():
        for h in range(2):
            finish(0, h, True)

    for t in (1, 2):
        for h in range(2):
            finish(t, h)

    for t in (1, 2):
        for h in range(2):
            reduce_sent(t, h)

    @pl.when(section == 0)
    def _():
        for h in range(2):
            reduce_sent(0, h)

    @pl.when(section == 1)
    def _():
        for h in range(2):
            reduce_sent(0, h, True)
            for j in range(RING):
                first_sum(h, j).wait_send()

    for b in range(blocks):
        rows_swap(b).wait_send()
    value_swap.wait_send()

    @pl.when(section == 0)
    def _():
        x_swap.wait_send()
        for which in range(2):
            for h in range(2):
                for d in range(2):
                    pass_copy(which, h, d).wait_send()
                    for p in range(2):
                        spread_copy(which, h, d, p).wait_send()

    @pl.when(section == 1)
    def _():
        g_swap.wait_send()
        for copy in deal_copies(0) + deal_copies(1):
            copy.wait_send()
        for t in range(3):
            for h in range(2):
                for d in range(2):
                    right_pass(t, h, d).wait_send()
                    for p in range(2):
                        right_copy(t, h, d, p).wait_send()
        for b in range(blocks):
            hop(b).wait_send()


def hand_out(*refs):
    sources, targets, sems = refs[:5], refs[5:10], refs[10]
    copies = [pltpu.make_async_copy(sources[i], targets[i], sems.at[i]) for i in range(5)]
    for copy in copies:
        copy.start()
    for copy in copies:
        copy.wait()


def per_device(layer_inputs, out_grad, w_gate, w_up, w_down, slot_token, slot_gate):
    tok, width = layer_inputs.shape[2:]
    hidden = w_gate.shape[2]
    slots_n = slot_token.shape[2]
    chunks = hidden // COLS
    rows_out = width // (NY * NZ * NX)
    vmem = pl.BlockSpec(memory_space=pltpu.VMEM)
    hbm = pl.BlockSpec(memory_space=pl.ANY)
    sem = pltpu.SemaphoreType.DMA
    grad = jax.ShapeDtypeStruct((1, rows_out, hidden), BF)
    shapes = (
        jax.ShapeDtypeStruct((1, 1, tok, width), BF), grad, grad, grad,
        jax.ShapeDtypeStruct((1, 1, slots_n), F32),
    )
    made = pl.pallas_call(
        body,
        out_shape=shapes,
        in_specs=[vmem, vmem, hbm, hbm, hbm, hbm, hbm],
        out_specs=(vmem,) * 5,
        scratch_shapes=[
            pltpu.VMEM((chunks, width, COLS), BF),
            pltpu.VMEM((chunks, width, COLS), BF),
            pltpu.VMEM((W2_RING, width, COLS), BF),
            pltpu.VMEM((2, tok, width), BF),
            pltpu.VMEM((2, tok, width), BF),
            pltpu.VMEM((slots_n, width), BF),
            pltpu.VMEM((2, RING * slots_n, width), BF),
            pltpu.VMEM((2, RING * slots_n, width), BF),
            pltpu.VMEM((RING, RING, 128, slots_n), BF),
            pltpu.VMEM((RING, RING, 128, slots_n), BF),
            pltpu.VMEM((3, chunks, RING * slots_n, COLS), BF),
            pltpu.VMEM((2, 2, RING, 128, RING * slots_n), BF),
            pltpu.VMEM((4, width // 4, slots_n), BF),
            pltpu.VMEM((4, width // 4, slots_n), BF),
            pltpu.VMEM((4, 2, tok, width // 4), BF),
            pltpu.VMEM((slots_n, 128), F32),
            pltpu.VMEM((slots_n, 128), F32),
            sem((2, chunks)), sem((W2_RING,)), sem((2,)),
            sem((3,)), sem((3,)), sem((4,)), sem((4,)), sem((4,)), sem((4,)),
            sem((2, 2, 3)), sem((2, 2, 3)), sem((3, 2, 2, 2)), sem((3, 2, 2, 2)), sem((3, 2, 2)), sem((3, 2, 2)),
            sem((2, 2, 2, 2)), sem((2, 2, 2, 2)), sem((2, 2, 2)), sem((2, 2, 2)),
            sem((3, 2, 3, 2)), sem((3, 2, 3, 2)), sem((3, 2, 2)), sem((3, 2, 2)),
            sem((2, RING)), sem((2, RING)),
            pltpu.SemaphoreType.REGULAR,
        ],
        compiler_params=pltpu.CompilerParams(
            collective_id=0, has_side_effects=True, vmem_limit_bytes=63 * 1024 * 1024),
    )(slot_token, slot_gate, layer_inputs, out_grad, w_gate, w_up, w_down)
    return pl.pallas_call(
        hand_out,
        out_shape=shapes,
        in_specs=[vmem] * 5,
        out_specs=(hbm,) * 5,
        scratch_shapes=[sem((5,))],
    )(*made)


def solution(mesh):
    placed = (
        P("section", None, ("dp", "et"), None),
        P(None, ("dp", "et"), None),
        P("section", None, "et"),
        P("section", None, "et"),
        P("section", None, "et"),
        P("section", None, "dp"),
        P("section", None, "dp"),
    )
    return jax.shard_map(
        per_device,
        mesh=mesh,
        in_specs=placed,
        out_specs=(
            P("section", None, ("dp", "et"), None),
            P("section", "dp", "et"),
            P("section", "dp", "et"),
            P("section", "dp", "et"),
            P("section", None, "dp"),
        ),
        check_vma=False,
    )
```

```python
import jax
import jax.numpy as jnp
from jax import lax
from jax.experimental import pallas as pl
from jax.experimental.pallas import tpu as pltpu
from jax.sharding import PartitionSpec as P

BF = jnp.bfloat16
F32 = jnp.float32
NY, NZ, NX = 4, 4, 2
RING = 4
COLS = 256
W2_RING = 5
MESH = pl.DeviceIdType.MESH


def dot(a, b):
    return jnp.dot(a, b, preferred_element_type=F32)


def dot_nt(a, b):
    return lax.dot_general(a, b, (((1,), (1,)), ((), ())), preferred_element_type=F32)


def body(
    slots_ref, gates_ref, x_hbm, g_hbm, w1_hbm, w3_hbm, w2_hbm,
    in_grad, gate_out, up_out, down_out, value_out,
    w1, w3, w2, x_full, g_full, g_rows, x_group, s_group,
    x_turned, s_turned, right, left, rows_mine, rows_theirs, grads_both,
    value_mine, value_theirs,
    load_sem, w2_sem, local_sem, pair_send, pair_recv, rows_send, rows_recv, hop_send, hop_recv,
    left_send, left_recv, right_send, right_recv, pass_send, pass_recv,
    group_send, group_recv, far_send, far_recv, sum_send, sum_recv, x_send, x_recv, first_send, first_recv, ready,
):
    section = lax.axis_index("section")
    et = lax.axis_index("et")
    dp = lax.axis_index("dp")
    z, y, x = dp // (NY * NX), (dp // NX) % NY, dp % NX
    slots_n = slots_ref.shape[2]
    tok = x_full.shape[1]
    chunks = w1.shape[0]
    half = chunks // 2
    ring_w2 = w2.shape[0]
    width = w1.shape[1]
    part_of = ((0, (half + 1) // 2), ((half + 1) // 2, half // 2))
    step_a = 1 + 2 * section
    step_b = 3 - 2 * section
    steps = (step_a, step_b)

    def at_y(step):
        return (section, et, z * (NY * NX) + ((y + step) % NY) * NX + x)

    def at_z(step):
        return (section, et, ((z + step) % NZ) * (NY * NX) + y * NX + x)

    pair = (section, 1 - et, dp)
    sibling = (1 - section, et, dp)
    x_peer = (section, et, z * (NY * NX) + y * NX + (1 - x))
    gather_to = (at_y, at_z)
    reduce_to = (at_z, at_y)
    gather_pos = (y, z)
    reduce_pos = (z, y)

    def remote(src, dst, send, recv, device):
        return pltpu.make_async_remote_copy(
            src_ref=src, dst_ref=dst, send_sem=send, recv_sem=recv,
            device_id=device, device_id_type=MESH)

    def w_load(hbm, ref, c, sem):
        start = pl.multiple_of(c * COLS, COLS)
        return pltpu.make_async_copy(hbm.at[0, :, pl.ds(start, COLS)], ref, sem)

    barrier = pltpu.get_barrier_semaphore()
    near = [x_peer] + [at_y(k) for k in (1, 3)] + [at_z(k) for k in (1, 3)]
    peers = [pair, sibling, at_y(2), at_z(2)] + near
    for peer in peers:
        pl.semaphore_signal(barrier, inc=1, device_id=peer, device_id_type=MESH)

    x_load = pltpu.make_async_copy(x_hbm.at[0, 0], x_full.at[0], local_sem.at[0])
    g_load = pltpu.make_async_copy(g_hbm.at[0], g_full.at[0], local_sem.at[1])
    x_load.start()

    @pl.when(section == 1)
    def _():
        g_load.start()

    @pl.loop(0, chunks)
    def _(c):
        w_load(w1_hbm, w1.at[c], c, load_sem.at[0, c]).start()
        w_load(w3_hbm, w3.at[c], c, load_sem.at[1, c]).start()

    @pl.loop(0, ring_w2)
    def _(c):
        w_load(w2_hbm, w2.at[c], c, w2_sem.at[c]).start()

    pl.semaphore_wait(barrier, len(peers))

    x_swap = remote(x_hbm.at[0, 0], x_full.at[1], pair_send.at[0], pair_recv.at[0], pair)
    g_swap = remote(g_hbm.at[0], g_full.at[1], pair_send.at[1], pair_recv.at[1], pair)

    x_swap.start()

    @pl.when(section == 1)
    def _():
        x_swap.wait_send()
        g_swap.start()

    def down_rows(row):
        return jnp.broadcast_to(row.astype(F32), (slots_n, slots_n)).T

    offsets = (et * tok, (1 - et) * tok)
    slot_rows = down_rows(slots_ref[0]).astype(jnp.int32)
    across = lax.broadcasted_iota(jnp.int32, (slots_n, tok), 1)
    pick = [jnp.where(slot_rows == across + o, 1.0, 0.0).astype(BF) for o in offsets]
    along = lax.broadcasted_iota(jnp.int32, (tok, slots_n), 0)
    place = [jnp.where(slots_ref[0] == along + o, 1.0, 0.0).astype(BF) for o in offsets]

    def turn(rows, into):
        for b in range(width // 128):
            block = rows[:, b * 128:(b + 1) * 128].astype(F32)
            into[b // 4, b % 4] = block.T.astype(BF)

    def deal_copies(which):
        source = (x_turned, s_turned)[which]
        copies = []
        for h in range(2):
            for k, step in ((2, 2), (1, step_a), (3, step_b)):
                there = (gather_pos[h] + step) % RING
                share = source.at[:, there] if h == 0 else source.at[there]
                copies.append(remote(share, left.at[which, h, :, :, pl.ds(k * 128, 128)],
                                     left_send.at[which, h, k - 1], left_recv.at[which, h, k - 1],
                                     gather_to[h](step)))
        return copies

    def deal(which):
        source = (x_turned, s_turned)[which]
        left[which, 0, :, :, 0:128] = source[:, gather_pos[0]]
        left[which, 1, :, :, 0:128] = source[gather_pos[1]]
        for copy in deal_copies(which):
            copy.start()

    def right_piece(t, h, p, k):
        start, count = part_of[p]
        return right.at[t, pl.ds(half * h + start, count), pl.ds(k * slots_n, slots_n), :]

    def right_copy(t, h, d, p):
        return remote(right_piece(t, h, p, 0), right_piece(t, h, p, 1 + 2 * d),
                      right_send.at[t, h, d, p], right_recv.at[t, h, d, p], gather_to[h](steps[d]))

    def right_pass(t, h, d):
        return remote(right_piece(t, h, d, 1 + 2 * d), right_piece(t, h, d, 2),
                      pass_send.at[t, h, d], pass_recv.at[t, h, d], gather_to[h](steps[d]))

    def right_spread(t):
        for d, p in ((0, 0), (1, 1), (0, 1), (1, 0)):
            for h in range(2):
                right_copy(t, h, d, p).start()

    def right_pass_on(t):
        for h in range(2):
            for d in range(2):
                right_copy(t, h, d, d).wait_recv()
                right_pass(t, h, d).start()

    def right_wait(t):
        for h in range(2):
            for d in range(2):
                right_copy(t, h, d, 1 - d).wait_recv()
                right_pass(t, h, d).wait_recv()

    groups = (x_group, s_group)
    span = width // 2

    def piece(which, h, p, k):
        return groups[which].at[h, pl.ds(k * slots_n, slots_n), pl.ds(p * span, span)]

    def spread_copy(which, h, d, p):
        return remote(piece(which, h, p, 0), piece(which, h, p, 1 + 2 * d),
                      group_send.at[which, h, d, p], group_recv.at[which, h, d, p], gather_to[h](steps[d]))

    def pass_copy(which, h, d):
        return remote(piece(which, h, d, 1 + 2 * d), piece(which, h, d, 2),
                      far_send.at[which, h, d], far_recv.at[which, h, d], gather_to[h](steps[d]))

    def spread(which):
        for d, p in ((0, 0), (1, 1), (0, 1), (1, 0)):
            for h in range(2):
                spread_copy(which, h, d, p).start()

    def pass_on(which):
        for h in range(2):
            for d in range(2):
                spread_copy(which, h, d, d).wait_recv()
                pass_copy(which, h, d).start()

    def group_wait(which):
        for h in range(2):
            for d in range(2):
                spread_copy(which, h, d, 1 - d).wait_recv()
                pass_copy(which, h, d).wait_recv()

    def left_make(which):
        for h in range(2):
            for j in range(RING):
                at = (j * RING + gather_pos[h]) if h == 0 else (gather_pos[h] * RING + j)
                cols = pl.ds(pl.multiple_of(at * 128, 128), 128)
                for k in range(RING):
                    tile = groups[which][h, k * slots_n:(k + 1) * slots_n, cols].astype(F32)
                    left[which, h, j, :, k * slots_n:(k + 1) * slots_n] = tile.T.astype(BF)

    own = pl.ds(0, slots_n)
    others = pl.ds(slots_n, (RING - 1) * slots_n)

    def forward(c, rows, at):
        pre_gate = dot(rows, w1[c])
        pre_up = dot(rows, w3[c])
        sigma = jax.nn.sigmoid(pre_gate)
        active = pre_gate * sigma
        right[0, c, at, :] = (active * pre_up).astype(BF)
        right[1, c, at, :] = (pre_up * sigma * (1.0 + pre_gate * (1.0 - sigma))).astype(BF)
        right[2, c, at, :] = active.astype(BF)

    def forward_others():
        group_wait(0)

        @pl.loop(0, chunks)
        def _(c):
            forward(c, x_group[c // half, others, :], others)

    def backward(c, scaled, at):
        for t in (1, 2):
            right[t, c, at, :] = (scaled * right[t, c, at, :].astype(F32)).astype(BF)

    def w2_load(i):
        return w_load(w2_hbm, w2.at[i % ring_w2], i % chunks, w2_sem.at[i % ring_w2])

    def w2_next(i):
        @pl.when(i + ring_w2 < (2 - section) * chunks)
        def _():
            w2_load(i + ring_w2).start()

    x_load.wait()
    x_swap.wait_recv()
    picked = (dot(pick[0], x_full[0]) + dot(pick[1], x_full[1])).astype(BF)
    for h in range(2):
        x_group[h, own, :] = picked
    @pl.when(section == 0)
    def _():
        spread(0)

    @pl.when(section == 1)
    def _():
        turn(x_group.at[0, own], x_turned)

    @pl.loop(0, chunks)
    def _(c):
        w_load(w1_hbm, w1.at[c], c, load_sem.at[0, c]).wait()
        w_load(w3_hbm, w3.at[c], c, load_sem.at[1, c]).wait()
        forward(c, x_group[0, own, :], own)

    blocks = grads_both.shape[0]
    step = width // blocks

    def hop(b):
        return remote(grads_both.at[b], g_full.at[:, :, pl.ds(b * step, step)],
                      hop_send.at[b], hop_recv.at[b], sibling)

    @pl.when(section == 1)
    def _():
        right_spread(0)
        g_load.wait()
        g_swap.wait_recv()

    @pl.when(section == 0)
    def _():
        pass_on(0)
        forward_others()
        left_make(0)

    gate_block = down_rows(gates_ref[0])
    gates = jnp.concatenate([gate_block] * (COLS // 128), axis=1)
    for b in range(blocks):
        cols = slice(b * step, (b + 1) * step)

        @pl.when(section == 0)
        def _():
            hop(b).wait_recv()

        rows = (dot(pick[0], g_full[0, :, cols]) + dot(pick[1], g_full[1, :, cols])).astype(BF)
        g_rows[:, cols] = rows
        scaled_rows = (jnp.concatenate([gate_block] * (step // 128), axis=1) * rows.astype(F32)).astype(BF)
        for h in range(2):
            s_group[h, own, cols] = scaled_rows

    @pl.when(section == 0)
    def _():
        spread(1)

    @pl.when(section == 1)
    def _():
        turn(s_group.at[0, own], s_turned)
        deal(1)
        deal(0)

    value_mine[...] = jnp.zeros_like(value_mine)

    @pl.loop(0, chunks)
    def _(c):
        w2_load(c).wait()
        back = dot(g_rows[...], w2[c % ring_w2])
        w2_next(c)
        product = right[0, c, own, :].astype(F32) * back
        value_mine[...] += product[:, :128] + product[:, 128:]
        backward(c, gates * back, own)

    @pl.when(section == 1)
    def _():
        right_spread(1)
        right_spread(2)

    value_swap = remote(value_mine, value_theirs, pair_send.at[2], pair_recv.at[2], pair)
    value_swap.start()

    def rows_swap(b):
        return remote(rows_mine.at[b], rows_theirs.at[b], rows_send.at[b], rows_recv.at[b], pair)

    @pl.loop(0, blocks)
    def _(b):
        at = pl.ds(pl.multiple_of(b * step, step), step)
        total_rows = jnp.zeros((step, slots_n), F32)
        for c in range(chunks):
            total_rows = (total_rows + dot_nt(w1[c, at, :], right[1, c, own, :])
                          + dot_nt(w3[c, at, :], right[2, c, own, :]))
        rows_mine[b] = total_rows.astype(BF)
        rows_swap(b).start()

        @pl.when((section == 0) & (b == 1))
        def _():
            pass_on(1)

    def token_grads(b, halves):
        rows_swap(b).wait_recv()
        cols = slice(b * step, (b + 1) * step)
        for i in halves:
            added = dot_nt(place[i], rows_mine[b]) + dot_nt(place[i], rows_theirs[b])
            grads_both[b, i] = (g_full[i, :, cols].astype(F32) + added).astype(BF)
        in_grad[0, 0, :, cols] = grads_both[b, 0]

    @pl.when(section == 1)
    def _():
        for b in range(blocks):
            token_grads(b, (0, 1))
            hop(b).start()

    @pl.when(section == 1)
    def _():
        right_pass_on(0)

    outs = (down_out, gate_out, up_out)
    block = RING * 128

    def multiply(t, h):
        which = 1 if t == 0 else 0

        @pl.loop(0, half)
        def _(n):
            c = half * h + n
            w1[c, t * block:(t + 1) * block, :] = dot(left[which, h].reshape(block, RING * slots_n), right[t, c]).astype(BF)

    def rows_at(t, row, side, early):
        count = 64 if early else 128
        at = t * block + row * 128 + (side * 64 if early else 0)
        return pl.ds(pl.multiple_of(at, 64), count)

    def part_at(t, h, p, row, early):
        start, count = part_of[p]
        return (pl.ds(half * h + start, count), rows_at(t, row, 0, early), slice(None))

    def of_block(t, h, p, step, early):
        start, count = part_of[p]
        return (pl.ds(half * h + start, count), rows_at(t, (reduce_pos[h] + step) % RING, x, early), slice(None))

    def first_sum(h, j):
        cols = pl.ds(half * h, half)
        return remote(w1.at[cols, pl.ds(pl.multiple_of(j * 128 + (1 - x) * 64, 64), 64), :],
                      w3.at[cols, pl.ds(j * 128 + 64, 64), :], first_send.at[h, j], first_recv.at[h, j], x_peer)

    def first_start(h):
        for j in range(RING):
            first_sum(h, j).start()

    def first_end(h):
        for j in range(RING):
            first_sum(h, j).wait_recv()
            cols = pl.ds(half * h, half)
            mine = (cols, pl.ds(pl.multiple_of(j * 128 + x * 64, 64), 64), slice(None))
            theirs = (cols, pl.ds(j * 128 + 64, 64), slice(None))
            w1[mine] = (w1[mine].astype(F32) + w3[theirs].astype(F32)).astype(BF)

    def far_sum(t, h, d, early):
        return remote(w1.at[of_block(t, h, d, 2, early)], w3.at[part_at(t, h, d, 2, early)],
                      sum_send.at[t, h, 0, d], sum_recv.at[t, h, 0, d], reduce_to[h](steps[d]))

    def near_sum(t, h, d, p, early):
        return remote(w1.at[of_block(t, h, p, steps[d], early)], w3.at[part_at(t, h, p, 1 + 2 * d, early)],
                      sum_send.at[t, h, 1 + p, d], sum_recv.at[t, h, 1 + p, d], reduce_to[h](steps[d]))

    def reduce_start(t, h, early=False):
        for d in range(2):
            far_sum(t, h, d, early).start()
        for d in range(2):
            near_sum(t, h, d, 1 - d, early).start()

    def merge(t, h, early=False):
        for d in range(2):
            far_sum(t, h, d, early).wait_recv()
            here = of_block(t, h, d, steps[d], early)
            w1[here] = (w1[here].astype(F32) + w3[part_at(t, h, d, 2, early)].astype(F32)).astype(BF)
            near_sum(t, h, d, d, early).start()

    def reduce_sent(t, h, early=False):
        for d in range(2):
            far_sum(t, h, d, early).wait_send()
            for p in range(2):
                near_sum(t, h, d, p, early).wait_send()
            if not early:
                x_copy(t, h, d).wait_send()

    def total(t, h, c, side, early):
        here = pl.multiple_of(t * block + reduce_pos[h] * 128 + side * 64, 64)
        value = w1[c, pl.ds(here, 64), :].astype(F32)
        for k in (1, 3):
            there = pl.multiple_of(t * block + k * 128 + (0 if early else side * 64), 64)
            value = value + w3[c, pl.ds(there, 64), :].astype(F32)
        return value

    def x_copy(t, h, p):
        start, count = part_of[p]
        at = (pl.ds(half * h + start, count), pl.ds(3 * block + t * 64, 64), slice(None))
        return remote(w1.at[at], w3.at[at], x_send.at[t, h, p], x_recv.at[t, h, p], x_peer)

    def near_wait(t, h, p, early):
        for d in range(2):
            near_sum(t, h, d, p, early).wait_recv()

    def reduce_end(t, h):
        for p in range(2):
            near_wait(t, h, p, False)
            start, count = part_of[p]

            @pl.loop(0, count)
            def _(n):
                c = half * h + start + n
                w1[c, 3 * block + t * 64:3 * block + (t + 1) * 64, :] = total(t, h, c, 1 - x, False).astype(BF)
            x_copy(t, h, p).start()

    def finish(t, h, early=False):
        for p in range(2):
            if early:
                near_wait(t, h, p, True)
            else:
                x_copy(t, h, p).wait_recv()
            start, count = part_of[p]
            for n in range(start, start + count):
                c = half * h + n
                value = total(t, h, c, x, early)
                if not early:
                    value = value + w3[c, 3 * block + t * 64:3 * block + (t + 1) * 64, :].astype(F32)
                outs[t][0, :, c * COLS:(c + 1) * COLS] = (value * (1.0 / 32.0)).astype(BF)

    for peer in near:
        pl.semaphore_signal(ready, inc=1, device_id=peer, device_id_type=MESH)

    @pl.when(section == 0)
    def _():
        group_wait(1)
        left_make(1)

    @pl.when(section == 1)
    def _():
        right_pass_on(1)
        for copy in deal_copies(1):
            copy.wait_recv()
        right_wait(0)

    multiply(0, 0)
    pl.semaphore_wait(ready, len(near))

    @pl.when(section == 0)
    def _():
        reduce_start(0, 0)

    @pl.when(section == 1)
    def _():
        first_start(0)
        right_pass_on(2)

    multiply(0, 1)

    @pl.when(section == 0)
    def _():
        reduce_start(0, 1)

        @pl.loop(0, chunks)
        def _(c):
            i = chunks + c
            w2_load(i).wait()
            scaled = dot(s_group[c // half, others, :], w2[i % ring_w2])
            w2_next(i)
            backward(c, scaled, others)

    @pl.when(section == 1)
    def _():
        first_start(1)
        for copy in deal_copies(0):
            copy.wait_recv()
        right_wait(1)

    multiply(1, 0)
    reduce_start(1, 0)

    @pl.when(section == 0)
    def _():
        merge(0, 0)

    multiply(1, 1)
    reduce_start(1, 1)

    @pl.when(section == 0)
    def _():
        merge(0, 1)

    @pl.when(section == 1)
    def _():
        right_wait(2)

    for h in range(2):
        multiply(2, h)
        reduce_start(2, h)
        merge(1, h)

    @pl.when(section == 0)
    def _():
        for h in range(2):
            reduce_end(0, h)
        for b in range(blocks):
            token_grads(b, (0,))

    for h in range(2):
        merge(2, h)

    @pl.when(section == 1)
    def _():
        for h in range(2):
            first_end(h)
            reduce_start(0, h, True)

    for h in range(2):
        reduce_end(1, h)

    @pl.when(section == 1)
    def _():
        for h in range(2):
            merge(0, h, True)

    value_swap.wait_recv()
    value_out[0] = jnp.sum((value_mine[...] + value_theirs[...]).T, axis=0, keepdims=True)

    @pl.when(section == 0)
    def _():
        for h in range(2):
            finish(0, h)

    for h in range(2):
        reduce_end(2, h)

    @pl.when(section == 1)
    def _():
        for h in range(2):
            finish(0, h, True)

    for t in (1, 2):
        for h in range(2):
            finish(t, h)

    for t in (1, 2):
        for h in range(2):
            reduce_sent(t, h)

    @pl.when(section == 0)
    def _():
        for h in range(2):
            reduce_sent(0, h)

    @pl.when(section == 1)
    def _():
        for h in range(2):
            reduce_sent(0, h, True)
            for j in range(RING):
                first_sum(h, j).wait_send()

    for b in range(blocks):
        rows_swap(b).wait_send()
    value_swap.wait_send()

    @pl.when(section == 0)
    def _():
        x_swap.wait_send()
        for which in range(2):
            for h in range(2):
                for d in range(2):
                    pass_copy(which, h, d).wait_send()
                    for p in range(2):
                        spread_copy(which, h, d, p).wait_send()

    @pl.when(section == 1)
    def _():
        g_swap.wait_send()
        for copy in deal_copies(0) + deal_copies(1):
            copy.wait_send()
        for t in range(3):
            for h in range(2):
                for d in range(2):
                    right_pass(t, h, d).wait_send()
                    for p in range(2):
                        right_copy(t, h, d, p).wait_send()
        for b in range(blocks):
            hop(b).wait_send()


def hand_out(*refs):
    sources, targets, sems = refs[:5], refs[5:10], refs[10]
    copies = [pltpu.make_async_copy(sources[i], targets[i], sems.at[i]) for i in range(5)]
    for copy in copies:
        copy.start()
    for copy in copies:
        copy.wait()


def per_device(layer_inputs, out_grad, w_gate, w_up, w_down, slot_token, slot_gate):
    tok, width = layer_inputs.shape[2:]
    hidden = w_gate.shape[2]
    slots_n = slot_token.shape[2]
    chunks = hidden // COLS
    rows_out = width // (NY * NZ * NX)
    vmem = pl.BlockSpec(memory_space=pltpu.VMEM)
    hbm = pl.BlockSpec(memory_space=pl.ANY)
    sem = pltpu.SemaphoreType.DMA
    grad = jax.ShapeDtypeStruct((1, rows_out, hidden), BF)
    shapes = (
        jax.ShapeDtypeStruct((1, 1, tok, width), BF), grad, grad, grad,
        jax.ShapeDtypeStruct((1, 1, slots_n), F32),
    )
    made = pl.pallas_call(
        body,
        out_shape=shapes,
        in_specs=[vmem, vmem, hbm, hbm, hbm, hbm, hbm],
        out_specs=(vmem,) * 5,
        scratch_shapes=[
            pltpu.VMEM((chunks, width, COLS), BF),
            pltpu.VMEM((chunks, width, COLS), BF),
            pltpu.VMEM((W2_RING, width, COLS), BF),
            pltpu.VMEM((2, tok, width), BF),
            pltpu.VMEM((2, tok, width), BF),
            pltpu.VMEM((slots_n, width), BF),
            pltpu.VMEM((2, RING * slots_n, width), BF),
            pltpu.VMEM((2, RING * slots_n, width), BF),
            pltpu.VMEM((RING, RING, 128, slots_n), BF),
            pltpu.VMEM((RING, RING, 128, slots_n), BF),
            pltpu.VMEM((3, chunks, RING * slots_n, COLS), BF),
            pltpu.VMEM((2, 2, RING, 128, RING * slots_n), BF),
            pltpu.VMEM((4, width // 4, slots_n), BF),
            pltpu.VMEM((4, width // 4, slots_n), BF),
            pltpu.VMEM((4, 2, tok, width // 4), BF),
            pltpu.VMEM((slots_n, 128), F32),
            pltpu.VMEM((slots_n, 128), F32),
            sem((2, chunks)), sem((W2_RING,)), sem((2,)),
            sem((3,)), sem((3,)), sem((4,)), sem((4,)), sem((4,)), sem((4,)),
            sem((2, 2, 3)), sem((2, 2, 3)), sem((3, 2, 2, 2)), sem((3, 2, 2, 2)), sem((3, 2, 2)), sem((3, 2, 2)),
            sem((2, 2, 2, 2)), sem((2, 2, 2, 2)), sem((2, 2, 2)), sem((2, 2, 2)),
            sem((3, 2, 3, 2)), sem((3, 2, 3, 2)), sem((3, 2, 2)), sem((3, 2, 2)),
            sem((2, RING)), sem((2, RING)),
            pltpu.SemaphoreType.REGULAR,
        ],
        compiler_params=pltpu.CompilerParams(
            collective_id=0, has_side_effects=True, vmem_limit_bytes=63 * 1024 * 1024),
    )(slot_token, slot_gate, layer_inputs, out_grad, w_gate, w_up, w_down)
    return pl.pallas_call(
        hand_out,
        out_shape=shapes,
        in_specs=[vmem] * 5,
        out_specs=(hbm,) * 5,
        scratch_shapes=[sem((5,))],
    )(*made)


def solution(mesh):
    placed = (
        P("section", None, ("dp", "et"), None),
        P(None, ("dp", "et"), None),
        P("section", None, "et"),
        P("section", None, "et"),
        P("section", None, "et"),
        P("section", None, "dp"),
        P("section", None, "dp"),
    )
    return jax.shard_map(
        per_device,
        mesh=mesh,
        in_specs=placed,
        out_specs=(
            P("section", None, ("dp", "et"), None),
            P("section", "dp", "et"),
            P("section", "dp", "et"),
            P("section", "dp", "et"),
            P("section", None, "dp"),
        ),
        check_vma=False,
    )
```
